32 devices in a mesh: gx: 8 (over z, y), gy: 4 (over x, core).
Axes of the slice: x: 2, y: 2, z: 4, core: 2. Of those that a mesh axis runs over, the one named last changes fastest.
Arguments:
- tokens: bfloat16 [65536, 768], P(('gx', 'gy'))
- seg_lengths: int32 [128, 4], P(('gx', 'gy')), may hold values from 1 to 256, 512 in all within a row
- cotangent: bfloat16 [65536, 768], P(('gx', 'gy')), may hold values from -6 to 6
- w_qkv: float32 [3, 768, 768], P(None, ('gx', 'gy')), may hold values from -0.21875 to 0.21875
- w_out: float32 [768, 768], P(('gx', 'gy')), may hold values from -0.875 to 0.875
- w_up: float32 [768, 3072], P(('gx', 'gy')), may hold values from -0.21875 to 0.21875
- w_down: float32 [3072, 768], P(('gx', 'gy')), may hold values from -0.109375 to 0.109375
- vecs: float32 [8, 768], P(None, ('gx', 'gy'))
- b_up: float32 [3072], P(('gx', 'gy')), may hold values from -1.8 to 1.8
- first_qkv: float32 [3, 768, 768], P(None, ('gx', 'gy')), may hold values from -1536 to 1536
- first_out: float32 [768, 768], P(('gx', 'gy')), may hold values from -1536 to 1536
- first_up: float32 [768, 3072], P(('gx', 'gy')), may hold values from -1536 to 1536
- first_down: float32 [3072, 768], P(('gx', 'gy')), may hold values from -1536 to 1536
- first_vecs: float32 [8, 768], P(None, ('gx', 'gy')), may hold values from -1536 to 1536
- first_bup: float32 [3072], P(('gx', 'gy')), may hold values from -1536 to 1536
- second_qkv: float32 [3, 768, 768], P(None, ('gx', 'gy')), may hold values from 32768 to 262144
- second_out: float32 [768, 768], P(('gx', 'gy')), may hold values from 32768 to 262144
- second_up: float32 [768, 3072], P(('gx', 'gy')), may hold values from 32768 to 262144
- second_down: float32 [3072, 768], P(('gx', 'gy')), may hold values from 32768 to 262144
- second_vecs: float32 [8, 768], P(None, ('gx', 'gy')), may hold values from 32768 to 262144
- second_bup: float32 [3072], P(('gx', 'gy')), may hold values from 32768 to 262144
- ema_qkv: float32 [3, 768, 768], P(None, ('gx', 'gy')), may hold values from -0.21875 to 0.21875
- ema_out: float32 [768, 768], P(('gx', 'gy')), may hold values from -0.875 to 0.875
- ema_up: float32 [768, 3072], P(('gx', 'gy')), may hold values from -0.21875 to 0.21875
- ema_down: float32 [3072, 768], P(('gx', 'gy')), may hold values from -0.109375 to 0.109375
- ema_vecs: float32 [8, 768], P(None, ('gx', 'gy'))
- ema_bup: float32 [3072], P(('gx', 'gy')), may hold values from -1.8 to 1.8
Outputs:
- layer_out: bfloat16 [65536, 768], P(('gx', 'gy'))
- grad_tokens: bfloat16 [65536, 768], P(('gx', 'gy'))
- new_qkv: float32 [3, 768, 768], P(None, ('gx', 'gy'))
- new_out: float32 [768, 768], P(('gx', 'gy'))
- new_up: float32 [768, 3072], P(('gx', 'gy'))
- new_down: float32 [3072, 768], P(('gx', 'gy'))
- new_vecs: float32 [8, 768], P(None, ('gx', 'gy'))
- new_bup: float32 [3072], P(('gx', 'gy'))
- firsts_qkv: float32 [3, 768, 768], P(None, ('gx', 'gy'))
- firsts_out: float32 [768, 768], P(('gx', 'gy'))
- firsts_up: float32 [768, 3072], P(('gx', 'gy'))
- firsts_down: float32 [3072, 768], P(('gx', 'gy'))
- firsts_vecs: float32 [8, 768], P(None, ('gx', 'gy'))
- firsts_bup: float32 [3072], P(('gx', 'gy'))
- seconds_qkv: float32 [3, 768, 768], P(None, ('gx', 'gy'))
- seconds_out: float32 [768, 768], P(('gx', 'gy'))
- seconds_up: float32 [768, 3072], P(('gx', 'gy'))
- seconds_down: float32 [3072, 768], P(('gx', 'gy'))
- seconds_vecs: float32 [8, 768], P(None, ('gx', 'gy'))
- seconds_bup: float32 [3072], P(('gx', 'gy'))
- ema_new_qkv: float32 [3, 768, 768], P(None, ('gx', 'gy'))
- ema_new_out: float32 [768, 768], P(('gx', 'gy'))
- ema_new_up: float32 [768, 3072], P(('gx', 'gy'))
- ema_new_down: float32 [3072, 768], P(('gx', 'gy'))
- ema_new_vecs: float32 [8, 768], P(None, ('gx', 'gy'))
- ema_new_bup: float32 [3072], P(('gx', 'gy'))
- copy_qkv: bfloat16 [3, 768, 768], P(None, ('gx', 'gy'))
- copy_out: bfloat16 [768, 768], P(('gx', 'gy'))
- copy_up: bfloat16 [768, 3072], P(('gx', 'gy'))
- copy_down: bfloat16 [3072, 768], P(('gx', 'gy'))
- copy_vecs: bfloat16 [8, 768], P(None, ('gx', 'gy'))
- copy_bup: bfloat16 [3072], P(('gx', 'gy'))
- trust_ratios: float32 [15], replicated
- norm_pairs: float32 [2, 15], replicated
The draws below stay inside these ranges and needn't reach their ends.
Inputs may be any that keep to these rules, and one draw needn't show every extreme that they name: `seg_lengths`: each row's 4 lengths are its pairs' token counts in order and sum to 512.
All inputs are finite; a program needn't handle non-finite values.
Results may differ from the reference program's by a relative error of at most 0.014.
The reference program's roundings to bfloat16 on the way count: a program that leaves them out, or rounds other values in their place, can miss the bound.
Values may be sent and summed in bfloat16 or wider, within the bound.
No kernel may reach another device: no remote copies, remote signals or barrier semaphores. Data moves between devices by JAX's collectives and lax.ppermute only.
A program may use at most 256 MiB of HBM per device.

```python
import math
import jax
import jax.numpy as jnp
import numpy as np
from jax import lax

D = 768
HEADS = 12
HD = 64
FF = 3072
LEN = 512
SEGS = 4
MOST = 256
STEP = 7
ROWS = 128
TOKENS = 65536


def gain_rows(key, low_end, top_ratio):
    columns = jnp.arange(D, dtype=jnp.float32) / D
    rising = low_end * jnp.exp(jnp.log(top_ratio) * columns)
    jitter = jax.random.uniform(key, (2, D), jnp.float32, 0.8, 1.25)
    return rising[None, :] * jitter


def assemble(biases, gains):
    return jnp.stack([biases[0], biases[1], biases[2], gains[0], biases[3], biases[4], gains[1], biases[5]])


def draw_tokens(key, part):
    key = jax.random.fold_in(key, 11)
    columns = jnp.arange(D, dtype=jnp.float32) / D
    rising = 0.6 * jnp.exp(jnp.log(3.0) * columns)
    values = jax.random.normal(key, (TOKENS, D), jnp.float32) * rising[None, :]
    return values.astype(jnp.bfloat16)


def draw_vecs(key, part):
    key = jax.random.fold_in(key, 21)
    biases = 0.3 * jax.random.normal(key, (6, D), jnp.float32)
    gains = gain_rows(jax.random.fold_in(key, 1), 0.6, 3.0)
    return assemble(biases, gains)


def draw_ema_vecs(key, part):
    key = jax.random.fold_in(key, 22)
    biases = 0.3 * jax.random.normal(key, (6, D), jnp.float32)
    gains = gain_rows(jax.random.fold_in(key, 1), 0.6, 3.0)
    return assemble(biases, gains)


def shard_levels(stream_key, shape, cuts, smallest, high):
    def one(axis_at, blocks):
        draws = jax.random.uniform(jax.random.fold_in(jax.random.fold_in(stream_key, 6), axis_at), (blocks,), jnp.float32, smallest / len(cuts), high / len(cuts))
        return jnp.repeat(jnp.exp(draws), shape[axis_at] // blocks).reshape((-1,) + (1,) * (len(shape) - axis_at - 1))

    level = one(*cuts[0])
    for cut in cuts[1:]:
        level = level * one(*cut)
    return level


def split_up(amount, total, reach, slope):
    weights = [(1 << 20) // math.isqrt(rank ** slope) + 1 for rank in range(2, amount + 1)]
    rest, holding = total - reach - (amount - 1), [1] * (amount - 1)
    while rest > 0:
        movable = [i for i in range(amount - 1) if holding[i] < reach]
        whole, left = sum([weights[i] for i in movable]), rest
        for i in movable:
            more = min(reach - holding[i], max(1, left * weights[i] // whole), rest)
            holding[i] = holding[i] + more
            rest = rest - more
    return np.array([reach] + holding)


def uneven(own_key, count, total, bound, skew):
    if count == 2:
        one = jax.random.randint(own_key, (), max(1, total - bound), min(bound, total - 1) + 1)
        return jnp.stack([one, total - one])
    lengths = jnp.asarray(split_up(count, total, bound, skew), jnp.int32)
    couples = (count - 1) // 2
    donor, sink = lengths[1:1 + 2 * couples:2], lengths[2:2 + 2 * couples:2]
    room = jnp.minimum(donor - 1, bound - sink)
    passed = jax.random.randint(jax.random.fold_in(own_key, 1), (couples,), 0, 1 << 20) % (room + 1)
    lengths = lengths.at[1:1 + 2 * couples:2].set(donor - passed).at[2:2 + 2 * couples:2].set(sink + passed)
    return lengths[jax.random.permutation(jax.random.fold_in(own_key, 2), count)]


def normal_values(own_key, dims, width, limit, split=(), kind=jnp.bfloat16):
    array = width * jax.random.normal(own_key, dims, jnp.float32)
    if split:
        array = array * shard_levels(own_key, dims, split, -0.22, 0.18)
    return jnp.clip(array, -limit, limit).astype(kind)


def setup_inputs(seed: int = 0) -> dict:
    arg_keys = jax.random.split(jax.random.key(seed), 28)
    tokens = draw_tokens(jax.random.fold_in(arg_keys[27], 71), 0)
    seg_lengths = jax.vmap(lambda own: uneven(own, SEGS, LEN, MOST, 2))(jax.random.split(arg_keys[1], ROWS)).reshape((ROWS, SEGS)).astype(jnp.int32)
    cotangent = normal_values(arg_keys[2], (TOKENS, D), 1.0, 6.0, ((0, 32),))
    w_qkv = normal_values(arg_keys[3], (3, D, D), D ** -0.5, 0.21875, ((1, 32),), jnp.float32)
    w_out = normal_values(arg_keys[4], (D, D), (D // 16) ** -0.5, 0.875, ((0, 32),), jnp.float32)
    w_up = normal_values(arg_keys[5], (D, FF), D ** -0.5, 0.21875, ((0, 32),), jnp.float32)
    w_down = normal_values(arg_keys[6], (FF, D), FF ** -0.5, 0.109375, ((0, 32),), jnp.float32)
    vecs = draw_vecs(jax.random.fold_in(arg_keys[27], 71), 0)
    b_up = normal_values(arg_keys[8], (FF,), 0.3, 1.8, ((0, 32),), jnp.float32)
    first_qkv = normal_values(arg_keys[9], (3, D, D), (TOKENS ** 0.5), 1536.0, ((1, 32),), jnp.float32)
    first_out = normal_values(arg_keys[10], (D, D), (TOKENS ** 0.5), 1536.0, ((0, 32),), jnp.float32)
    first_up = normal_values(arg_keys[11], (D, FF), (TOKENS ** 0.5), 1536.0, ((0, 32),), jnp.float32)
    first_down = normal_values(arg_keys[12], (FF, D), (TOKENS ** 0.5), 1536.0, ((0, 32),), jnp.float32)
    first_vecs = normal_values(arg_keys[13], (8, D), (TOKENS ** 0.5), 1536.0, ((1, 32),), jnp.float32)
    first_bup = normal_values(arg_keys[14], (FF,), (TOKENS ** 0.5), 1536.0, ((0, 32),), jnp.float32)
    second_qkv = jnp.clip(jnp.exp(math.log(262144.0) - 2.0794415 * jax.random.uniform(arg_keys[15], (3, D, D), jnp.float32) ** shard_levels(arg_keys[15], (3, D, D), ((1, 32),), -0.2, 0.2)), 32768.0, 262144.0)
    second_out = jnp.clip(jnp.exp(math.log(262144.0) - 2.0794415 * jax.random.uniform(arg_keys[16], (D, D), jnp.float32) ** shard_levels(arg_keys[16], (D, D), ((0, 32),), -0.2, 0.2)), 32768.0, 262144.0)
    second_up = jnp.clip(jnp.exp(math.log(262144.0) - 2.0794415 * jax.random.uniform(arg_keys[17], (D, FF), jnp.float32) ** shard_levels(arg_keys[17], (D, FF), ((0, 32),), -0.2, 0.2)), 32768.0, 262144.0)
    second_down = jnp.clip(jnp.exp(math.log(262144.0) - 2.0794415 * jax.random.uniform(arg_keys[18], (FF, D), jnp.float32) ** shard_levels(arg_keys[18], (FF, D), ((0, 32),), -0.2, 0.2)), 32768.0, 262144.0)
    second_vecs = jnp.clip(jnp.exp(math.log(262144.0) - 2.0794415 * jax.random.uniform(arg_keys[19], (8, D), jnp.float32) ** shard_levels(arg_keys[19], (8, D), ((1, 32),), -0.2, 0.2)), 32768.0, 262144.0)
    second_bup = jnp.clip(jnp.exp(math.log(262144.0) - 2.0794415 * jax.random.uniform(arg_keys[20], (FF,), jnp.float32) ** shard_levels(arg_keys[20], (FF,), ((0, 32),), -0.2, 0.2)), 32768.0, 262144.0)
    ema_qkv = normal_values(arg_keys[21], (3, D, D), D ** -0.5, 0.21875, ((1, 32),), jnp.float32)
    ema_out = normal_values(arg_keys[22], (D, D), (D // 16) ** -0.5, 0.875, ((0, 32),), jnp.float32)
    ema_up = normal_values(arg_keys[23], (D, FF), D ** -0.5, 0.21875, ((0, 32),), jnp.float32)
    ema_down = normal_values(arg_keys[24], (FF, D), FF ** -0.5, 0.109375, ((0, 32),), jnp.float32)
    ema_vecs = draw_ema_vecs(jax.random.fold_in(arg_keys[27], 71), 0)
    ema_bup = normal_values(arg_keys[26], (FF,), 0.3, 1.8, ((0, 32),), jnp.float32)
    return {"tokens": tokens, "seg_lengths": seg_lengths, "cotangent": cotangent, "w_qkv": w_qkv, "w_out": w_out, "w_up": w_up, "w_down": w_down, "vecs": vecs, "b_up": b_up, "first_qkv": first_qkv, "first_out": first_out, "first_up": first_up, "first_down": first_down, "first_vecs": first_vecs, "first_bup": first_bup, "second_qkv": second_qkv, "second_out": second_out, "second_up": second_up, "second_down": second_down, "second_vecs": second_vecs, "second_bup": second_bup, "ema_qkv": ema_qkv, "ema_out": ema_out, "ema_up": ema_up, "ema_down": ema_down, "ema_vecs": ema_vecs, "ema_bup": ema_bup}


@jax.custom_vjp
def low(v):
    return lax.optimization_barrier(v.astype(jnp.bfloat16)).astype(jnp.float32)

@jax.custom_vjp
def low_back(v):
    return v

def low_keep(v):
    return (low(v), None)

def low_pass(kept, grad):
    return (grad,)

def back_keep(v):
    return (v, None)

def back_low(kept, grad):
    return (low(grad),)
low.defvjp(low_keep, low_pass)
low_back.defvjp(back_keep, back_low)
highest = lax.Precision.HIGHEST
norm_eps = 1e-12
beta_one = 0.5
beta_two = 0.5
adam_eps = 1e-06
decay_rate = 0.01
learn_rate = 0.3
ema_rate = 0.5
ratio_eps = 1e-06

def layer_norm(values, gain_row, bias_row):
    center = values - lax.optimization_barrier(jnp.mean(values, axis=-1, keepdims=True))
    spread = lax.optimization_barrier(jnp.mean(center * center, axis=-1, keepdims=True))
    return center * lax.rsqrt(spread + norm_eps) * gain_row + bias_row

def segment_ids(seg_lengths):
    bounds = jnp.cumsum(seg_lengths, axis=1).astype(jnp.int32)
    places = jnp.arange(LEN, dtype=jnp.int32)
    return lax.optimization_barrier(jnp.sum((places[None, :, None] >= bounds[:, None, :]).astype(jnp.int32), axis=2))

def attend_row(inputs):
    queries, key_rows, value_rows, seg_row = inputs
    queries = queries.reshape(LEN, HEADS, HD)
    key_rows = key_rows.reshape(LEN, HEADS, HD)
    value_rows = value_rows.reshape(LEN, HEADS, HD)
    same_seg = seg_row[:, None] == seg_row[None, :]
    raw_scores = jnp.einsum('qhd,khd->hqk', queries, key_rows, precision=highest)
    scores = low_back(raw_scores * HD ** (-0.5))
    masked = jnp.where(same_seg[None], scores, -1e+30)
    attn_probs = low(jax.nn.softmax(masked, axis=-1))
    mixed = jnp.einsum('hqk,khd->qhd', attn_probs, value_rows, precision=highest)
    return mixed.reshape(LEN, D)

def forward(tokens, w_qkv, w_out, w_up, w_down, vecs, b_up, seg_ids):
    bias_qkv = jnp.stack([vecs[0], jnp.zeros_like(vecs[0]), vecs[1]])
    projected = jnp.einsum('td,sde->ste', tokens, w_qkv, precision=highest) + bias_qkv[:, None, :]
    projected = low(low_back(projected))
    shaped = projected.reshape(3, ROWS, LEN, D)
    mixed = lax.map(jax.checkpoint(attend_row), (shaped[0], shaped[1], shaped[2], seg_ids))
    mixed = low(low_back(mixed.reshape(TOKENS, D)))
    attn_out = low_back(jnp.dot(mixed, w_out, precision=highest) + vecs[2])
    hidden = layer_norm(tokens + attn_out, vecs[3], vecs[4])
    pre_act = low_back(jnp.dot(low(hidden), w_up, precision=highest) + b_up)
    active = low(jax.nn.gelu(pre_act, approximate=False))
    ffn_out = low_back(jnp.dot(active, w_down, precision=highest) + vecs[5])
    return layer_norm(hidden + ffn_out, vecs[6], vecs[7])

def tensor_squares(tensors):
    return jnp.concatenate([lax.optimization_barrier(jnp.sum(tensors[0] * tensors[0], axis=(1, 2))), jnp.sum(tensors[1] * tensors[1])[None], jnp.sum(tensors[2] * tensors[2])[None], jnp.sum(tensors[3] * tensors[3])[None], lax.optimization_barrier(jnp.sum(tensors[4] * tensors[4], axis=1)), jnp.sum(tensors[5] * tensors[5])[None]])

def spread_ratios(ratios):
    return (ratios[0:3][:, None, None], ratios[3], ratios[4], ratios[5], ratios[6:14][:, None], ratios[14])

def reference(tokens, seg_lengths, cotangent, w_qkv, w_out, w_up, w_down, vecs, b_up, first_qkv, first_out, first_up, first_down, first_vecs, first_bup, second_qkv, second_out, second_up, second_down, second_vecs, second_bup, ema_qkv, ema_out, ema_up, ema_down, ema_vecs, ema_bup):
    seg_ids = segment_ids(seg_lengths)
    masters = (w_qkv, w_out, w_up, w_down, vecs, b_up)

    def layer(token_vals, copy_a, copy_b, copy_c, copy_d, copy_e, copy_f):
        return forward(token_vals, copy_a, copy_b, copy_c, copy_d, copy_e, copy_f, seg_ids)
    result, pullback = jax.vjp(layer, tokens.astype(jnp.float32), low(w_qkv), low(w_out), low(w_up), low(w_down), low(vecs), low(b_up))
    grads = pullback(cotangent.astype(jnp.float32))
    grad_input = grads[0]
    reduced = grads[1:]
    firsts_in = (first_qkv, first_out, first_up, first_down, first_vecs, first_bup)
    seconds_in = (second_qkv, second_out, second_up, second_down, second_vecs, second_bup)
    averages = (ema_qkv, ema_out, ema_up, ema_down, ema_vecs, ema_bup)
    corr_one = 1.0 - beta_one ** STEP
    corr_two = 1.0 - beta_two ** STEP
    firsts = []
    seconds = []
    updates = []
    for member in range(6):
        first_new = beta_one * firsts_in[member] + (1.0 - beta_one) * reduced[member]
        second_new = beta_two * seconds_in[member] + (1.0 - beta_two) * reduced[member] * reduced[member]
        update = first_new / corr_one / (jnp.sqrt(second_new / corr_two) + adam_eps) + decay_rate * masters[member]
        firsts.append(first_new)
        seconds.append(second_new)
        updates.append(update)
    sq_weight = tensor_squares(masters)
    sq_update = tensor_squares(updates)
    ratios = jnp.sqrt(sq_weight) / jnp.sqrt(sq_update + ratio_eps)
    scales = spread_ratios(ratios)
    renewed = [masters[member] - learn_rate * scales[member] * updates[member] for member in range(6)]
    emas = [ema_rate * averages[member] + (1.0 - ema_rate) * renewed[member] for member in range(6)]
    norm_pairs = jnp.stack([jnp.sqrt(sq_weight), jnp.sqrt(sq_update)])
    return (result.astype(jnp.bfloat16), grad_input.astype(jnp.bfloat16), renewed[0], renewed[1], renewed[2], renewed[3], renewed[4], renewed[5], firsts[0], firsts[1], firsts[2], firsts[3], firsts[4], firsts[5], seconds[0], seconds[1], seconds[2], seconds[3], seconds[4], seconds[5], emas[0], emas[1], emas[2], emas[3], emas[4], emas[5], renewed[0].astype(jnp.bfloat16), renewed[1].astype(jnp.bfloat16), renewed[2].astype(jnp.bfloat16), renewed[3].astype(jnp.bfloat16), renewed[4].astype(jnp.bfloat16), renewed[5].astype(jnp.bfloat16), ratios, norm_pairs)
```

```python
import functools

import jax
import jax.numpy as jnp
from jax import lax
from jax.experimental import pallas as pl
from jax.experimental.pallas import tpu as pltpu
from jax.sharding import PartitionSpec as P

STEP = 7
ALL = ("gx", "gy")
norm_eps = 1e-12
beta_one = 0.5
beta_two = 0.5
adam_eps = 1e-06
decay_rate = 0.01
learn_rate = 0.3
ema_rate = 0.5
ratio_eps = 1e-06

HEADS = 12
HD = 64
PAIR = 2 * HD
MASKED = -1e30
CHIPS = 16
MIB = 1 << 20
f32 = jnp.float32
bf16 = jnp.bfloat16
NT = (((1,), (1,)), ((), ()))
NN = (((1,), (0,)), ((), ()))
TN = (((0,), (0,)), ((), ()))


def dot(a, b, dims=NN):
    return lax.dot_general(a, b, dims, preferred_element_type=f32)


def seg_of(bounds_ref, row, shape, dim):
    place = lax.broadcasted_iota(jnp.int32, shape, dim)
    total = jnp.zeros(shape, jnp.int32)
    for k in range(bounds_ref.shape[1]):
        total += (place >= bounds_ref[row, k]).astype(jnp.int32)
    return total


def seg_columns(bounds_ref, row, length):
    shape = (length, PAIR)
    seg = seg_of(bounds_ref, row, shape, 0)
    lane = lax.broadcasted_iota(jnp.int32, shape, 1)
    low = lane < HD
    spot = jnp.where(low, lane, lane - HD)
    same = spot == seg
    inside = spot < 4
    query_cols = jnp.where(same, 1.0, 0.0).astype(bf16)
    key_cols = jnp.where(inside, jnp.where(same, 0.0, MASKED), 0.0).astype(bf16)
    return low, query_cols, key_cols


def load_qkv(where_ref, raws, w_scr, sem):
    chip, core = where_ref[0], where_ref[1]
    half = w_scr.shape[2] // 2
    copies = []
    for side in range(2):
        col = pl.multiple_of((core if side == 0 else 1 - core) * half, PAIR)
        for xy in range(4):
            raw = raws[side * 4 + xy]
            for z in range(4):
                at = where_ref[2 + xy * 4 + z]
                rows = w_scr.shape[1] // CHIPS
                for s in range(3):
                    copies.append(
                        pltpu.make_async_copy(
                            raw.at[pl.ds((3 * z + s) * rows, rows), :],
                            w_scr.at[s, pl.ds(pl.multiple_of(at * rows, 16), rows), pl.ds(col, half)],
                            sem,
                        )
                    )
    for c in copies:
        c.start()
    for c in copies:
        c.wait()


def key_span(block, step, reach, length):
    first = max(0, block * step - (reach - 1)) // step * step
    last = min(length, -(-((block + 1) * step - 1 + reach) // step) * step)
    return first, last


def attend_forward_kernel(
    where_ref, bounds_ref, x_ref, vec_ref, *rest
):
    raws = rest[:8]
    qkv_ref, o_ref, lse_ref, wout_ref, w_scr, qkv_scr, sem, out_sem = rest[8:]
    row = pl.program_id(0)
    length = x_ref.shape[0]
    width = x_ref.shape[1]

    @pl.when(row == 0)
    def _():
        load_qkv(where_ref, raws, w_scr, sem)
        pltpu.make_async_copy(w_scr, wout_ref, out_sem).start()

    x = x_ref[...]
    q = (dot(x, w_scr[0]) + vec_ref[0:1, :]).astype(bf16) * jnp.asarray(HD**-0.5, bf16)
    qkv_scr[:, 0:width] = q
    qkv_scr[:, width : 2 * width] = dot(x, w_scr[1]).astype(bf16)
    qkv_scr[:, 2 * width : 3 * width] = (dot(x, w_scr[2]) + vec_ref[1:2, :]).astype(bf16)
    qkv_ref[...] = qkv_scr[...]
    low, query_cols, key_cols = seg_columns(bounds_ref, row, length)
    sub = lax.broadcasted_iota(jnp.int32, (PAIR, length), 0)
    step = 128
    reach = 256

    def pair_body(pair, _):
        at = pl.multiple_of(pair * PAIR, PAIR)
        qp = qkv_scr[:, pl.ds(at, PAIR)]
        kp = qkv_scr[:, pl.ds(width + at, PAIR)]
        vt = qkv_scr[:, pl.ds(2 * width + at, PAIR)].T
        outs = []
        logs = []
        for even in (True, False):
            pick = low if even else jnp.logical_not(low)
            qa = jnp.where(pick, qp, query_cols)
            ka = jnp.where(pick, kp, key_cols)
            if even:
                va = jnp.where(sub < HD, vt, (sub == HD).astype(bf16))
            else:
                va = jnp.where(sub < HD, (sub == 0).astype(bf16), vt)
            blocks = []
            lse_blocks = []
            for b in range(length // step):
                first, last = key_span(b, step, reach, length)
                scores = dot(ka[first:last], qa[b * step : (b + 1) * step], NT)
                peak = jnp.max(scores, axis=0, keepdims=True)
                probs = jnp.exp(scores - peak).astype(bf16)
                mixed = dot(va[:, first:last], probs)
                total = mixed[HD : HD + 1] if even else mixed[0:1]
                mine = mixed[:HD] if even else mixed[HD:]
                blocks.append((mine * (1.0 / total)).astype(bf16))
                lse_blocks.append(peak + jnp.log(total))
            outs.append(jnp.concatenate(blocks, axis=1))
            logs.append(jnp.concatenate(lse_blocks, axis=1))
        o_ref[:, pl.ds(at, PAIR)] = jnp.concatenate(outs, axis=0).T
        lse_ref[0, pl.ds(pair, 1)] = jnp.concatenate(logs, axis=0)[None]
        return 0

    lax.fori_loop(0, width // PAIR, pair_body, 0, unroll=True)

    @pl.when(row == pl.num_programs(0) - 1)
    def _():
        pltpu.make_async_copy(w_scr, wout_ref, out_sem).wait()


def attend_forward(where, bounds, tokens, vec_rows, raws):
    rows = bounds.shape[0]
    tok, width = tokens.shape
    length = tok // rows
    pairs = width // PAIR
    any_spec = pl.BlockSpec(memory_space=pl.ANY)
    return pl.pallas_call(
        attend_forward_kernel,
        grid_spec=pltpu.PrefetchScalarGridSpec(
            num_scalar_prefetch=2,
            grid=(rows,),
            in_specs=[
                pl.BlockSpec((length, width), lambda r, *_: (r, 0)),
                pl.BlockSpec(vec_rows.shape, lambda r, *_: (0, 0)),
            ]
            + [any_spec] * 8,
            out_specs=[
                pl.BlockSpec((length, 3 * width), lambda r, *_: (r, 0)),
                pl.BlockSpec((length, width), lambda r, *_: (r, 0)),
                pl.BlockSpec((1, pairs, 2, length), lambda r, *_: (r, 0, 0, 0)),
                any_spec,
            ],
            scratch_shapes=[
                pltpu.VMEM((3, width, width), bf16),
                pltpu.VMEM((length, 3 * width), bf16),
                pltpu.SemaphoreType.DMA,
                pltpu.SemaphoreType.DMA,
            ],
        ),
        out_shape=[
            jax.ShapeDtypeStruct((tok, 3 * width), bf16),
            jax.ShapeDtypeStruct((tok, width), bf16),
            jax.ShapeDtypeStruct((rows, pairs, 2, length), f32),
            jax.ShapeDtypeStruct((3, width, width), bf16),
        ],
        compiler_params=pltpu.CompilerParams(vmem_limit_bytes=56 * MIB),
        name="attend_forward",
    )(where, bounds, tokens, vec_rows, *raws)


def lane_mean(v):
    return jnp.mean(v, axis=1, keepdims=True)


def norm_parts(v):
    center = v - lane_mean(v)
    scale = lax.rsqrt(lane_mean(center * center) + 1e-12)
    return center * scale, scale


def norm_back(grad, unit, scale, gain):
    grad_unit = grad * gain
    return scale * (grad_unit - lane_mean(grad_unit) - unit * lane_mean(grad_unit * unit))


def fold(v):
    return jnp.sum(v.reshape(v.shape[0] // 8, 8, v.shape[1]), axis=0)


def gelu_both(z):
    size = jnp.abs(z)
    t = pl.reciprocal(1.0 + (0.3275911 * 0.5**0.5) * size, approx=APPROX)
    e = jnp.exp(-0.5 * z * z)
    poly = 0.5 * 1.061405429
    for a in (-1.453152027, 1.421413741, -0.284496736, 0.254829592):
        poly = poly * t + 0.5 * a
    tail = poly * t * e
    cdf = jnp.where(z >= 0, 1.0 - tail, tail)
    return z * cdf, cdf + z * e * 0.3989422804014327


APPROX = False
FC = 768
SLOTS = 4


def middle_kernel(
    where_ref, mixed_ref, x_ref, cot_ref, vec_ref, packed_ref,
    out_ref, gmixed_ref, gres_ref, gvec_ref, mine_a, theirs_a, mine_b, theirs_b,
    w1, w2, wo, acc1, acc2, acco, accv, act, slope, stage_a, stage_b, in_sem, out_sem,
):
    step = pl.program_id(0)
    width = x_ref.shape[1]
    chunks = w1.shape[1] // width

    @pl.when(step == 0)
    def _():
        copies = [pltpu.make_async_copy(packed_ref.at[:, pl.ds(2 * chunks * width, width)], wo, in_sem)]
        copies.append(pltpu.make_async_copy(packed_ref.at[:, pl.ds(0, chunks * width)], w1, in_sem))
        for j in range(chunks):
            copies.append(
                pltpu.make_async_copy(
                    packed_ref.at[:, pl.ds((chunks + j) * width, width)], w2.at[pl.ds(j * width, width), :], in_sem
                )
            )
        for c in copies:
            c.start()
        acc1[...] = jnp.zeros_like(acc1)
        acc2[...] = jnp.zeros_like(acc2)
        acco[...] = jnp.zeros_like(acco)
        accv[...] = jnp.zeros_like(accv)
        for c in copies:
            c.wait()

    mixed = mixed_ref[...]
    res_one = x_ref[...].astype(f32) + dot(mixed, wo[...]) + vec_ref[2:3, :]
    unit_one, scale_one = norm_parts(res_one)
    hidden = unit_one * vec_ref[3:4, :] + vec_ref[4:5, :]
    hidden_low = hidden.astype(bf16)
    ffn = hidden + vec_ref[5:6, :]
    for j in range(w1.shape[1] // FC):
        cols = slice(j * FC, (j + 1) * FC)
        at = j * FC // width
        inner = slice(j * FC - at * width, (j + 1) * FC - at * width)
        z = dot(hidden_low, w1[:, cols]) + vec_ref[8 + at : 9 + at, inner]
        g, d = gelu_both(z)
        g = g.astype(bf16)
        act[:, cols] = g
        slope[:, cols] = d.astype(slope.dtype)
        ffn += dot(g, w2[cols, :])
    unit_two, scale_two = norm_parts(ffn)
    out_ref[...] = (unit_two * vec_ref[6:7, :] + vec_ref[7:8, :]).astype(bf16)
    grad = cot_ref[...].astype(f32)
    accv[6] += fold(grad * unit_two)
    accv[7] += fold(grad)
    grad_two = norm_back(grad, unit_two, scale_two, vec_ref[6:7, :])
    grad_ffn = grad_two.astype(bf16)
    accv[5] += fold(grad_ffn.astype(f32))
    grad_hidden = grad_two
    hidden_t = hidden_low.T
    for j in range(w1.shape[1] // FC):
        cols = slice(j * FC, (j + 1) * FC)
        at = j * FC // width
        inner = slice(j * FC - at * width, (j + 1) * FC - at * width)
        gz = (dot(grad_ffn, w2[cols, :], NT) * slope[:, cols].astype(f32)).astype(bf16)
        accv[8 + at, :, inner] += fold(gz.astype(f32))
        acc2[cols, :] += dot(act[:, cols], grad_ffn, TN)
        acc1[:, cols] += dot(hidden_t, gz)
        grad_hidden += dot(gz, w1[:, cols], NT)
    accv[3] += fold(grad_hidden * unit_one)
    accv[4] += fold(grad_hidden)
    grad_one = norm_back(grad_hidden, unit_one, scale_one, vec_ref[3:4, :])
    gres_ref[...] = grad_one
    grad_attn = grad_one.astype(bf16)
    accv[2] += fold(grad_attn.astype(f32))
    acco[...] += dot(mixed, grad_attn, TN)
    gmixed_ref[...] = dot(grad_attn, wo[...], NT).astype(bf16)

    @pl.when(step == pl.num_programs(0) - 1)
    def _():
        gvec_ref[...] = jnp.sum(accv[...], axis=1)
        part = stage_a.shape[1]
        amount = mine_a.shape[0]

        def send(n, side, dst_a, dst_b, wait):
            core = where_ref[1] if side == 0 else 1 - where_ref[1]
            row = pl.multiple_of((where_ref[2 + n] * 2 + core) * part, 8)
            rows = pl.ds(row, part)
            slot = side + 2 * lax.rem(n, SLOTS)
            copy_a = pltpu.make_async_copy(stage_a.at[slot], dst_a.at[n], out_sem.at[slot, 0])
            copy_b = pltpu.make_async_copy(stage_b.at[slot], dst_b.at[n], out_sem.at[slot, 1])

            @pl.when(wait)
            def _():
                copy_a.wait()
                copy_b.wait()

            stage_a[slot] = acc1[rows, :].astype(bf16)
            for j in range(chunks):
                stage_b[slot, :, j * width : (j + 1) * width] = acc2[
                    pl.ds(pl.multiple_of(j * width + row, 8), part), :
                ].astype(bf16)
            stage_b[slot, :, chunks * width :] = acco[rows, :].astype(bf16)
            copy_a.start()
            copy_b.start()
            return copy_a, copy_b

        def body(n, _):
            send(n, 1, theirs_a, theirs_b, n >= SLOTS)
            send(n, 0, mine_a, mine_b, n >= SLOTS)
            return 0

        lax.fori_loop(0, amount, body, 0)
        for slot in range(2 * SLOTS):
            pltpu.make_async_copy(stage_a.at[slot], mine_a.at[0], out_sem.at[slot, 0]).wait()
            pltpu.make_async_copy(stage_b.at[slot], mine_b.at[0], out_sem.at[slot, 1]).wait()


def middle(where, mixed, tokens, cotangent, vec_rows, packed, block=256):
    tok, width = tokens.shape
    chunks = (packed.shape[1] // width - 1) // 2
    chips = CHIPS
    part = width // (2 * chips)
    any_spec = pl.BlockSpec(memory_space=pl.ANY)
    row_spec = pl.BlockSpec((block, width), lambda r, *_: (r, 0))
    vec_spec = pl.BlockSpec((vec_rows.shape[0], width), lambda r, *_: (0, 0))
    ff = chunks * width
    return pl.pallas_call(
        middle_kernel,
        grid_spec=pltpu.PrefetchScalarGridSpec(
            num_scalar_prefetch=1,
            grid=(tok // block,),
            in_specs=[row_spec, row_spec, row_spec, vec_spec, any_spec],
            out_specs=[row_spec, row_spec, row_spec, vec_spec] + [any_spec] * 4,
            scratch_shapes=[
                pltpu.VMEM((width, ff), bf16),
                pltpu.VMEM((ff, width), bf16),
                pltpu.VMEM((width, width), bf16),
                pltpu.VMEM((width, ff), f32),
                pltpu.VMEM((ff, width), f32),
                pltpu.VMEM((width, width), f32),
                pltpu.VMEM((vec_rows.shape[0], 8, width), f32),
                pltpu.VMEM((block, ff), bf16),
                pltpu.VMEM((block, ff), bf16),
                pltpu.VMEM((2 * SLOTS, part, ff), bf16),
                pltpu.VMEM((2 * SLOTS, part, ff + width), bf16),
                pltpu.SemaphoreType.DMA,
                pltpu.SemaphoreType.DMA((2 * SLOTS, 2)),
            ],
        ),
        out_shape=[
            jax.ShapeDtypeStruct((tok, width), bf16),
            jax.ShapeDtypeStruct((tok, width), bf16),
            jax.ShapeDtypeStruct((tok, width), f32),
            jax.ShapeDtypeStruct(vec_rows.shape, f32),
            jax.ShapeDtypeStruct((chips, part, ff), bf16),
            jax.ShapeDtypeStruct((chips, part, ff), bf16),
            jax.ShapeDtypeStruct((chips, part, ff + width), bf16),
            jax.ShapeDtypeStruct((chips, part, ff + width), bf16),
        ],
        compiler_params=pltpu.CompilerParams(vmem_limit_bytes=60 * MIB),
        name="middle",
    )(where, mixed, tokens, cotangent, vec_rows, packed)


def attend_backward_kernel(
    where_ref, bounds_ref, x_ref, q_ref, k_ref, v_ref, mixed_ref, gmixed_ref, lse_ref,
    gqkv_ref, gbias_ref, mine_ref, theirs_ref,
    acc, accb, probs_scr, grads_scr, stage, out_sem,
):
    row = pl.program_id(0)
    length, width = q_ref.shape
    pairs = width // PAIR
    low, query_cols, key_cols = seg_columns(bounds_ref, row, length)
    step = 128
    reach = 256

    @pl.when(row == 0)
    def _():
        acc[...] = jnp.zeros_like(acc)
        accb[...] = jnp.zeros_like(accb)
        probs_scr[...] = jnp.zeros_like(probs_scr)
        grads_scr[...] = jnp.zeros_like(grads_scr)

    head_of = lax.broadcasted_iota(jnp.int32, (8, width), 1) // HD
    pick_head = (head_of == lax.broadcasted_iota(jnp.int32, (8, width), 0)).astype(bf16)
    product = gmixed_ref[...].astype(f32) * mixed_ref[...].astype(f32)
    upper = product.astype(bf16)
    lower = (product - upper.astype(f32)).astype(bf16)
    means = dot(pick_head, upper, NT) + dot(pick_head, lower, NT)
    none = jnp.zeros((length, PAIR), bf16)

    for pair in range(pairs):
        at = slice(pair * PAIR, (pair + 1) * PAIR)
        qp, kp, vp, gp = q_ref[:, at], k_ref[:, at], v_ref[:, at], gmixed_ref[:, at]
        kt = kp.T
        for side in range(2):
            pick = low if side == 0 else jnp.logical_not(low)
            qa = jnp.where(pick, qp, query_cols)
            ka = jnp.where(pick, kp, key_cols)
            va = jnp.where(pick, vp, none)
            for b in range(length // step):
                first, last = key_span(b, step, reach, length)
                block = slice(b * step, (b + 1) * step)
                cols = slice(side * length + b * step, side * length + (b + 1) * step)
                scores = dot(ka[first:last], qa[block], NT)
                probs = jnp.exp(scores - lse_ref[0, pair, side : side + 1, block])
                gprobs = dot(va[first:last], gp[block], NT)
                head = 2 * pair + side
                grads = probs * (gprobs - means[head : head + 1, block])
                probs_scr[first:last, cols] = probs.astype(bf16)
                grads_scr[first:last, cols] = grads.astype(bf16)
        gq_t = jnp.concatenate(
            [dot(kt[:HD], grads_scr[:, :length]), dot(kt[HD:], grads_scr[:, length:])], axis=0
        )
        gq = (gq_t * HD**-0.5).astype(bf16).T
        both_q = jnp.concatenate([jnp.where(low, qp, none), jnp.where(low, none, qp)], axis=0)
        both_g = jnp.concatenate([jnp.where(low, gp, none), jnp.where(low, none, gp)], axis=0)
        gk = dot(grads_scr[...], both_q).astype(bf16)
        gv = dot(probs_scr[...], both_g).astype(bf16)
        for s, part in enumerate((gq, gk, gv)):
            spot = slice(s * width + pair * PAIR, s * width + (pair + 1) * PAIR)
            gqkv_ref[:, spot] = part
            if s != 1:
                accb[:, spot] += fold(part.astype(f32))
    acc[...] += dot(x_ref[...], gqkv_ref[...], TN)

    @pl.when(row == pl.num_programs(0) - 1)
    def _():
        gbias_ref[...] = jnp.broadcast_to(jnp.sum(accb[...], axis=0, keepdims=True), gbias_ref.shape)
        part = stage.shape[1]
        amount = mine_ref.shape[0]

        def send(n, side, dst):
            core = where_ref[1] if side == 0 else 1 - where_ref[1]
            rows = pl.ds(pl.multiple_of((where_ref[2 + n] * 2 + core) * part, 8), part)
            slot = side * amount + n
            stage[slot] = acc[rows, :].astype(bf16)
            pltpu.make_async_copy(stage.at[slot], dst.at[n], out_sem).start()

        def body(n, _):
            send(n, 1, theirs_ref)
            send(n, 0, mine_ref)
            return 0

        lax.fori_loop(0, amount, body, 0)
        pltpu.make_async_copy(stage.at[pl.ds(0, amount)], mine_ref, out_sem).wait()
        pltpu.make_async_copy(stage.at[pl.ds(amount, amount)], theirs_ref, out_sem).wait()


def attend_backward(where, bounds, tokens, qkv, mixed, gmixed, lse, group, groups):
    rows = bounds.shape[0]
    tok, model = tokens.shape
    length = tok // rows
    width = model // groups
    pairs = width // PAIR
    chips = CHIPS
    part = model // (2 * chips)
    any_spec = pl.BlockSpec(memory_space=pl.ANY)
    own = lambda s: pl.BlockSpec((length, width), lambda r, *_: (r, s * groups + group))
    return pl.pallas_call(
        attend_backward_kernel,
        grid_spec=pltpu.PrefetchScalarGridSpec(
            num_scalar_prefetch=2,
            grid=(rows,),
            in_specs=[
                pl.BlockSpec((length, model), lambda r, *_: (r, 0)),
                own(0), own(1), own(2), own(0), own(0),
                pl.BlockSpec((1, pairs, 2, length), lambda r, *_: (r, group, 0, 0)),
            ],
            out_specs=[
                pl.BlockSpec((length, 3 * width), lambda r, *_: (r, 0)),
                pl.BlockSpec((8, 3 * width), lambda r, *_: (0, 0)),
                any_spec,
                any_spec,
            ],
            scratch_shapes=[
                pltpu.VMEM((model, 3 * width), f32),
                pltpu.VMEM((8, 3 * width), f32),
                pltpu.VMEM((length, 2 * length), bf16),
                pltpu.VMEM((length, 2 * length), bf16),
                pltpu.VMEM((2 * chips, part, 3 * width), bf16),
                pltpu.SemaphoreType.DMA,
            ],
        ),
        out_shape=[
            jax.ShapeDtypeStruct((tok, 3 * width), bf16),
            jax.ShapeDtypeStruct((8, 3 * width), f32),
            jax.ShapeDtypeStruct((chips, part, 3 * width), bf16),
            jax.ShapeDtypeStruct((chips, part, 3 * width), bf16),
        ],
        compiler_params=pltpu.CompilerParams(vmem_limit_bytes=56 * MIB),
        name="attend_backward",
    )(where, bounds, tokens, qkv, qkv, qkv, mixed, gmixed, lse)


def input_grad_kernel(gres_ref, w_ref, *rest):
    parts, out_ref = rest[:-1], rest[-1]
    total = gres_ref[...]
    width = parts[0].shape[1] // 3
    for g, part in enumerate(parts):
        for s in range(3):
            total += dot(part[:, s * width : (s + 1) * width], w_ref[s, :, g * width : (g + 1) * width], NT)
    out_ref[...] = total.astype(bf16)


def input_grad(gres, weights, parts, block=512):
    tok, model = gres.shape
    return pl.pallas_call(
        input_grad_kernel,
        grid=(tok // block,),
        in_specs=[
            pl.BlockSpec((block, model), lambda r: (r, 0)),
            pl.BlockSpec(weights.shape, lambda r: (0, 0, 0)),
        ]
        + [pl.BlockSpec((block, p.shape[1]), lambda r: (r, 0)) for p in parts],
        out_specs=pl.BlockSpec((block, model), lambda r: (r, 0)),
        out_shape=jax.ShapeDtypeStruct((tok, model), bf16),
        compiler_params=pltpu.CompilerParams(vmem_limit_bytes=56 * MIB),
        name="input_grad",
    )(gres, weights, *parts)


class Ring:
    def __init__(self, sizes):
        self.sizes = sizes
        self.amount = sizes["gx"] * sizes["gy"]
        self.near = sizes == {"gx": 8, "gy": 4}

    def index(self):
        return lax.axis_index("gx") * self.sizes["gy"] + lax.axis_index("gy")

    def swap(self, value, bits):
        return lax.ppermute(value, ALL, [(i, i ^ bits) for i in range(self.amount)])

    def core(self, value):
        return self.swap(value, 1)

    def plane(self, value, k):
        return self.swap(value, k << 1)

    def line(self, value, k):
        return self.swap(value, k << 3)


def where_am_i(ring):
    if not ring.near:
        return jnp.asarray([0, 0] + list(range(CHIPS)), jnp.int32)
    me = ring.index()
    chip = me // 2
    order = [chip ^ ((z << 2) | xy) for xy in range(4) for z in range(4)]
    return jnp.stack([chip, me % 2] + order).astype(jnp.int32)


def gather_first(ring, w_qkv, vec_part):
    low = w_qkv.astype(bf16)
    part, width = low.shape[1], low.shape[2]
    half = width // 2
    vec_rows = vec_part.shape[0]
    vec_part = vec_part.astype(bf16)
    if not ring.near:
        full = lax.all_gather(low, ALL, axis=1, tiled=True)
        blocks = full.reshape(3, CHIPS, width // CHIPS, 2, half).transpose(3, 1, 0, 2, 4)
        blocks = blocks.reshape(8, 4 * 3 * width // CHIPS, half)
        vecs = lax.all_gather(vec_part, ALL, axis=1, tiled=True)
        return [blocks[i] for i in range(8)], vecs.astype(f32)
    me = ring.index()
    core = me % 2
    spread = jnp.zeros((16, width), bf16)
    spread = lax.dynamic_update_slice(spread, vec_part, (0, me * part))
    spread = spread.reshape(32, half)
    left, right = low[:, :, :half], low[:, :, half:]
    keep = jnp.where(core == 0, left, right)
    give = jnp.where(core == 0, right, left)
    got = ring.core(jnp.concatenate([give.reshape(3 * part, half), spread], axis=0))
    came = got[: 3 * part].reshape(3, part, half)
    block = jnp.where(
        core == 0, jnp.concatenate([keep, came], axis=1), jnp.concatenate([came, keep], axis=1)
    ).reshape(6 * part, half)
    payload = jnp.concatenate([block, spread + got[3 * part :]], axis=0)
    cut = 6 * part
    lines = [payload] + [ring.line(payload, k) for k in (1, 2, 3)]
    total = lines[0][cut:] + lines[1][cut:] + lines[2][cut:] + lines[3][cut:]
    payload = jnp.concatenate([v[:cut] for v in lines] + [total], axis=0)
    mine = [payload] + [ring.plane(payload, k) for k in (1, 2, 3)]
    theirs = [ring.core(v) for v in mine]
    cut = 4 * cut
    total = mine[0][cut:] + mine[1][cut:] + mine[2][cut:] + mine[3][cut:]
    return mine + theirs, total.reshape(16, width)[:vec_rows].astype(f32)


def gather_rest(w_out, w_up, w_down):
    part, width = w_out.shape
    chunks = w_up.shape[1] // width
    up = w_up.astype(bf16).reshape(part, width, chunks).transpose(0, 2, 1).reshape(part, chunks * width)
    down = w_down.astype(bf16).reshape(part, chunks * width)
    packed = jnp.concatenate([up, down, w_out.astype(bf16)], axis=1)
    return lax.all_gather(packed, ALL, axis=0, tiled=True)


def scatter(ring, mine, theirs, vec=None):
    chips, part, width = mine.shape
    if not ring.near:
        full = jnp.stack([mine, theirs], axis=1).reshape(2 * chips * part, width)
        total = lax.psum_scatter(full, ALL, scatter_dimension=0, tiled=True).astype(f32)
        if vec is not None:
            vec = lax.psum(vec, ALL)
        return total, vec
    came = ring.core(theirs)
    if vec is not None:
        vec = vec + ring.core(vec)

    def packed(rows, vec):
        rows = rows.astype(bf16).reshape(-1, width)
        if vec is None:
            return rows
        return jnp.concatenate([rows, vec.reshape(-1, width).astype(bf16)], axis=0)

    def added(rows, vec, parts):
        cut = rows.shape[0] * rows.shape[1]
        for p in parts:
            rows = rows + p[:cut].reshape(rows.shape).astype(f32)
            if vec is not None:
                vec = vec + p[cut:].reshape(vec.shape).astype(f32)
        return rows, vec

    def near(xy):
        at = slice(4 * xy, 4 * xy + 4)
        return mine[at].astype(f32) + came[at].astype(f32)

    parts = [ring.plane(packed(near(k), vec), k) for k in (1, 2, 3)]
    rows, vec = added(near(0), vec, parts)
    parts = [ring.line(packed(rows[k : k + 1], vec), k) for k in (1, 2, 3)]
    rows, vec = added(rows[:1], vec, parts)
    return rows[0], vec


def sum_small(ring, values):
    if not ring.near:
        return lax.psum(values, ALL)
    row = jnp.zeros((1, 128), f32).at[0, : values.shape[0]].set(values)
    spread = jnp.broadcast_to(row[None], (ring.amount, 1, 128))
    came = lax.all_to_all(spread, ALL, 0, 0)
    return jnp.sum(came, axis=(0, 1))[: values.shape[0]]


def tensor_squares(tensors):
    return jnp.concatenate(
        [
            jnp.sum(tensors[0] * tensors[0], axis=(1, 2)),
            jnp.sum(tensors[1] * tensors[1])[None],
            jnp.sum(tensors[2] * tensors[2])[None],
            jnp.sum(tensors[3] * tensors[3])[None],
            jnp.sum(tensors[4] * tensors[4], axis=1),
            jnp.sum(tensors[5] * tensors[5])[None],
        ]
    )


def spread_ratios(ratios):
    return (
        ratios[0:3][:, None, None],
        ratios[3],
        ratios[4],
        ratios[5],
        ratios[6:14][:, None],
        ratios[14],
    )


GROUPS = 2


def on_device(
    ring,
    tokens,
    seg_lengths,
    cotangent,
    *params,
):
    masters = params[0:6]
    firsts_in = params[6:12]
    seconds_in = params[12:18]
    averages = params[18:24]
    w_qkv, w_out, w_up, w_down, vecs, b_up = masters
    part, width = w_out.shape
    chunks = w_up.shape[1] // width
    bounds = jnp.stack(
        [jnp.sum(seg_lengths[:, : k + 1], axis=1) for k in range(seg_lengths.shape[1])], axis=1
    ).astype(jnp.int32)
    where = where_am_i(ring)
    packed = gather_rest(w_out, w_up, w_down)
    vec_part = jnp.concatenate([vecs, b_up.reshape(part, chunks).T], axis=0)
    raws, vec_rows = gather_first(ring, w_qkv, vec_part)
    vec_rows = jnp.concatenate([vec_rows, jnp.zeros((4, width), f32)], axis=0)
    qkv, mixed, lse, full_qkv = attend_forward(where, bounds, tokens, vec_rows, raws)
    layer_out, gmixed, gres, gvec, mine_a, theirs_a, mine_b, theirs_b = middle(
        where, mixed, tokens, cotangent, vec_rows, packed
    )
    grad_up, _ = scatter(ring, mine_a, theirs_a)
    grad_rest, _ = scatter(ring, mine_b, theirs_b)
    backs = [
        attend_backward(where, bounds, tokens, qkv, mixed, gmixed, lse, g, GROUPS) for g in range(GROUPS)
    ]
    grad_input = input_grad(gres, full_qkv, [b[0] for b in backs])
    own = width // GROUPS
    gbias = jnp.concatenate([b[1][0].reshape(3, own) for b in backs], axis=1)
    gvec = jnp.concatenate([gbias[0:1], gbias[2:3], gvec[2:12]], axis=0)
    sums = []
    for g, b in enumerate(backs):
        total, back_vec = scatter(ring, b[2], b[3], gvec if g == GROUPS - 1 else None)
        sums.append(total.reshape(part, 3, own))
    grad_qkv = jnp.concatenate(sums, axis=2).transpose(1, 0, 2)
    gvec = lax.dynamic_slice(back_vec, (0, ring.index() * part), (12, part))
    ff = chunks * width
    reduced = (
        grad_qkv,
        grad_rest[:, ff:],
        grad_up.reshape(part, chunks, width).transpose(0, 2, 1).reshape(part, ff),
        grad_rest[:, :ff].reshape(part * chunks, width),
        gvec[:8],
        gvec[8:].T.reshape(part * chunks),
    )
    corr_one = 1.0 - beta_one**STEP
    corr_two = 1.0 - beta_two**STEP
    firsts = []
    seconds = []
    updates = []
    for member in range(6):
        first_new = beta_one * firsts_in[member] + (1.0 - beta_one) * reduced[member]
        second_new = (
            beta_two * seconds_in[member] + (1.0 - beta_two) * reduced[member] * reduced[member]
        )
        update = (
            first_new / corr_one / (jnp.sqrt(second_new / corr_two) + adam_eps)
            + decay_rate * masters[member]
        )
        firsts.append(first_new)
        seconds.append(second_new)
        updates.append(update)
    squares = sum_small(ring, jnp.concatenate([tensor_squares(masters), tensor_squares(updates)]))
    sq_weight, sq_update = squares[:15], squares[15:]
    ratios = jnp.sqrt(sq_weight) / jnp.sqrt(sq_update + ratio_eps)
    scales = spread_ratios(ratios)
    renewed = [
        masters[member] - learn_rate * scales[member] * updates[member] for member in range(6)
    ]
    emas = [ema_rate * averages[member] + (1.0 - ema_rate) * renewed[member] for member in range(6)]
    norm_pairs = jnp.stack([jnp.sqrt(sq_weight), jnp.sqrt(sq_update)])
    copies = [v.astype(bf16) for v in renewed]
    return (layer_out, grad_input, *renewed, *firsts, *seconds, *emas, *copies, ratios, norm_pairs)


def solution(mesh):
    ring = Ring(dict(mesh.shape))
    rows = P(ALL, None)
    kinds = (P(None, ALL, None), rows, rows, rows, P(None, ALL), P(ALL))
    return jax.shard_map(
        functools.partial(on_device, ring),
        mesh=mesh,
        in_specs=(rows, rows, rows) + kinds * 4,
        out_specs=(rows, rows) + kinds * 5 + (P(), P()),
        check_vma=False,
    )
```

```python
import functools

import jax
import jax.numpy as jnp
from jax import lax
from jax.experimental import pallas as pl
from jax.experimental.pallas import tpu as pltpu
from jax.sharding import PartitionSpec as P

ALL = ("gx", "gy")

HEADS = 12
HD = 64
PAIR = 2 * HD
MASKED = -1e30
CHIPS = 16
MIB = 1 << 20
f32 = jnp.float32
bf16 = jnp.bfloat16
NT = (((1,), (1,)), ((), ()))
NN = (((1,), (0,)), ((), ()))
TN = (((0,), (0,)), ((), ()))


def dot(a, b, dims=NN):
    return lax.dot_general(a, b, dims, preferred_element_type=f32)


def cost(us):
    return pl.CostEstimate(flops=int(us * 1.1e9), bytes_accessed=int(us * 1e6), transcendentals=0)


def seg_of(bounds_ref, row, shape, dim):
    place = lax.broadcasted_iota(jnp.int32, shape, dim)
    total = jnp.zeros(shape, jnp.int32)
    for k in range(bounds_ref.shape[1]):
        total += (place >= bounds_ref[row, k]).astype(jnp.int32)
    return total


def seg_columns(bounds_ref, row, length):
    shape = (length, PAIR)
    seg = seg_of(bounds_ref, row, shape, 0)
    lane = lax.broadcasted_iota(jnp.int32, shape, 1)
    low = lane < HD
    spot = jnp.where(low, lane, lane - HD)
    same = spot == seg
    inside = spot < 4
    query_cols = jnp.where(same, 1.0, 0.0).astype(bf16)
    key_cols = jnp.where(inside, jnp.where(same, 0.0, MASKED), 0.0).astype(bf16)
    return low, query_cols, key_cols


def load_qkv(where_ref, raws, w_scr, sem):
    chip, core = where_ref[0], where_ref[1]
    half = w_scr.shape[2] // 2
    copies = []
    for side in range(2):
        col = pl.multiple_of((core if side == 0 else 1 - core) * half, PAIR)
        for xy in range(4):
            raw = raws[side * 4 + xy]
            for z in range(4):
                at = where_ref[2 + xy * 4 + z]
                rows = w_scr.shape[1] // CHIPS
                for s in range(3):
                    copies.append(
                        pltpu.make_async_copy(
                            raw.at[pl.ds((3 * z + s) * rows, rows), :],
                            w_scr.at[s, pl.ds(pl.multiple_of(at * rows, 16), rows), pl.ds(col, half)],
                            sem,
                        )
                    )
    for c in copies:
        c.start()
    for c in copies:
        c.wait()


def key_span(block, step, reach, length):
    first = max(0, block * step - (reach - 1)) // step * step
    last = min(length, -(-((block + 1) * step - 1 + reach) // step) * step)
    return first, last


def attend_forward_kernel(
    where_ref, bounds_ref, x_ref, vec_ref, *rest
):
    raws = rest[:8]
    qkv_ref, o_ref, probs_ref, share_ref, wout_ref, w_scr, qkv_scr, sem, out_sem = rest[8:]
    row = pl.program_id(0)
    length = x_ref.shape[0]
    width = x_ref.shape[1]

    @pl.when(row == 0)
    def _():
        load_qkv(where_ref, raws, w_scr, sem)
        pltpu.make_async_copy(w_scr, wout_ref, out_sem).start()

    x = x_ref[...]
    q = (dot(x, w_scr[0]) + vec_ref[0:1, :]).astype(bf16) * jnp.asarray(HD**-0.5, bf16)
    qkv_scr[:, 0:width] = q
    qkv_scr[:, width : 2 * width] = dot(x, w_scr[1]).astype(bf16)
    qkv_scr[:, 2 * width : 3 * width] = (dot(x, w_scr[2]) + vec_ref[1:2, :]).astype(bf16)
    qkv_ref[...] = qkv_scr[...]
    low, query_cols, key_cols = seg_columns(bounds_ref, row, length)
    sub = lax.broadcasted_iota(jnp.int32, (PAIR, length), 0)
    step = 128
    reach = 256

    def pair_body(pair, _):
        at = pl.multiple_of(pair * PAIR, PAIR)
        qp = qkv_scr[:, pl.ds(at, PAIR)]
        kp = qkv_scr[:, pl.ds(width + at, PAIR)]
        vt = qkv_scr[:, pl.ds(2 * width + at, PAIR)].T
        outs = []
        tops = []
        for side in range(2):
            pick = low if side == 0 else jnp.logical_not(low)
            qa = jnp.where(pick, qp, query_cols)
            ka = jnp.where(pick, kp, key_cols)
            if side == 0:
                va = jnp.where(sub < HD, vt, (sub == HD).astype(bf16))
            else:
                va = jnp.where(sub < HD, (sub == 0).astype(bf16), vt)
            blocks = []
            shares = []
            for b in range(length // step):
                first, last = key_span(b, step, reach, length)
                scores = dot(ka[first:last], qa[b * step : (b + 1) * step], NT)
                peak = jnp.max(scores, axis=0, keepdims=True)
                probs = jnp.exp(scores - peak).astype(bf16)
                cols = slice(side * length + b * step, side * length + (b + 1) * step)
                probs_ref[0, pair, first:last, cols] = probs
                if first > 0:
                    probs_ref[0, pair, 0:first, cols] = jnp.zeros((first, step), bf16)
                if last < length:
                    probs_ref[0, pair, last:length, cols] = jnp.zeros((length - last, step), bf16)
                mixed = dot(va[:, first:last], probs)
                total = mixed[HD : HD + 1] if side == 0 else mixed[0:1]
                mine = mixed[:HD] if side == 0 else mixed[HD:]
                share = 1.0 / total
                blocks.append((mine * share).astype(bf16))
                shares.append(share)
            outs.append(jnp.concatenate(blocks, axis=1))
            tops.append(jnp.concatenate(shares, axis=1))
        o_ref[:, pl.ds(at, PAIR)] = jnp.concatenate(outs, axis=0).T
        share_ref[0, pl.ds(pair, 1)] = jnp.concatenate(tops, axis=0)[None]
        return 0

    lax.fori_loop(0, width // PAIR, pair_body, 0, unroll=True)

    @pl.when(row == pl.num_programs(0) - 1)
    def _():
        pltpu.make_async_copy(w_scr, wout_ref, out_sem).wait()


def attend_forward(where, bounds, tokens, vec_rows, raws):
    rows = bounds.shape[0]
    tok, width = tokens.shape
    length = tok // rows
    pairs = width // PAIR
    any_spec = pl.BlockSpec(memory_space=pl.ANY)
    return pl.pallas_call(
        attend_forward_kernel,
        grid_spec=pltpu.PrefetchScalarGridSpec(
            num_scalar_prefetch=2,
            grid=(rows,),
            in_specs=[
                pl.BlockSpec((length, width), lambda r, *_: (r, 0)),
                pl.BlockSpec(vec_rows.shape, lambda r, *_: (0, 0)),
            ]
            + [any_spec] * 8,
            out_specs=[
                pl.BlockSpec((length, 3 * width), lambda r, *_: (r, 0)),
                pl.BlockSpec((length, width), lambda r, *_: (r, 0)),
                pl.BlockSpec((1, pairs, length, 2 * length), lambda r, *_: (r, 0, 0, 0)),
                pl.BlockSpec((1, pairs, 2, length), lambda r, *_: (r, 0, 0, 0)),
                any_spec,
            ],
            scratch_shapes=[
                pltpu.VMEM((3, width, width), bf16),
                pltpu.VMEM((length, 3 * width), bf16),
                pltpu.SemaphoreType.DMA,
                pltpu.SemaphoreType.DMA,
            ],
        ),
        out_shape=[
            jax.ShapeDtypeStruct((tok, 3 * width), bf16),
            jax.ShapeDtypeStruct((tok, width), bf16),
            jax.ShapeDtypeStruct((rows, pairs, length, 2 * length), bf16),
            jax.ShapeDtypeStruct((rows, pairs, 2, length), f32),
            jax.ShapeDtypeStruct((3, width, width), bf16),
        ],
        compiler_params=pltpu.CompilerParams(vmem_limit_bytes=56 * MIB),
        cost_estimate=cost(30),
        name="attend_forward",
    )(where, bounds, tokens, vec_rows, *raws)


def lane_mean(v):
    return jnp.mean(v, axis=1, keepdims=True)


def norm_parts(v):
    center = v - lane_mean(v)
    scale = lax.rsqrt(lane_mean(center * center) + 1e-12)
    return center * scale, scale


def norm_back(grad, unit, scale, gain):
    grad_unit = grad * gain
    return scale * (grad_unit - lane_mean(grad_unit) - unit * lane_mean(grad_unit * unit))


def fold(v):
    return jnp.sum(v.reshape(v.shape[0] // 8, 8, v.shape[1]), axis=0)


def gelu_both(z):
    size = jnp.abs(z)
    t = pl.reciprocal(1.0 + (0.3275911 * 0.5**0.5) * size, approx=False)
    e = jnp.exp(-0.5 * z * z)
    poly = 0.5 * 1.061405429
    for a in (-1.453152027, 1.421413741, -0.284496736, 0.254829592):
        poly = poly * t + 0.5 * a
    tail = poly * t * e
    cdf = jnp.where(z >= 0, 1.0 - tail, tail)
    return z * cdf, cdf + z * e * 0.3989422804014327


SLOTS = 4
EARLY = 3


def middle_kernel(
    where_ref, mixed_ref, x_ref, cot_ref, vec_ref, packed_ref,
    out_ref, gmixed_ref, gres_ref, gvec_ref, down_ref, mine_ref, theirs_0, theirs_1, theirs_2, theirs_3,
    w1, w2, wo, acc1, acc2, acco, accv, act, slope, stage, tall, in_sem, out_sem, tall_sem,
):
    step = pl.program_id(0)
    width = x_ref.shape[1]
    chunks = w1.shape[1] // width

    @pl.when(step == 0)
    def _():
        copies = [pltpu.make_async_copy(packed_ref.at[:, pl.ds(2 * chunks * width, width)], wo, in_sem)]
        copies.append(pltpu.make_async_copy(packed_ref.at[:, pl.ds(0, chunks * width)], w1, in_sem))
        for j in range(chunks):
            copies.append(
                pltpu.make_async_copy(
                    packed_ref.at[:, pl.ds((chunks + j) * width, width)], w2.at[pl.ds(j * width, width), :], in_sem
                )
            )
        for c in copies:
            c.start()
        acc1[...] = jnp.zeros_like(acc1)
        acc2[...] = jnp.zeros_like(acc2)
        acco[...] = jnp.zeros_like(acco)
        accv[...] = jnp.zeros_like(accv)
        for c in copies:
            c.wait()

    mixed = mixed_ref[...]
    res_one = x_ref[...].astype(f32) + dot(mixed, wo[...]) + vec_ref[2:3, :]
    unit_one, scale_one = norm_parts(res_one)
    hidden = unit_one * vec_ref[3:4, :] + vec_ref[4:5, :]
    hidden_low = hidden.astype(bf16)
    ffn = hidden + vec_ref[5:6, :]
    z = dot(hidden_low, w1[:, 0:width]) + vec_ref[8:9, :]
    for j in range(chunks):
        cols = slice(j * width, (j + 1) * width)
        if j + 1 < chunks:
            z_next = dot(hidden_low, w1[:, (j + 1) * width : (j + 2) * width]) + vec_ref[9 + j : 10 + j, :]
        g, d = gelu_both(z)
        g = g.astype(bf16)
        act[:, cols] = g
        slope[:, cols] = d.astype(slope.dtype)
        ffn += dot(g, w2[cols, :])
        z = z_next
    unit_two, scale_two = norm_parts(ffn)
    out_ref[...] = (unit_two * vec_ref[6:7, :] + vec_ref[7:8, :]).astype(bf16)
    grad = cot_ref[...].astype(f32)
    accv[6] += fold(grad * unit_two)
    accv[7] += fold(grad)
    grad_two = norm_back(grad, unit_two, scale_two, vec_ref[6:7, :])
    grad_ffn = grad_two.astype(bf16)
    accv[5] += fold(grad_ffn.astype(f32))
    grad_hidden = grad_two
    hidden_t = hidden_low.T
    for j in range(chunks):
        cols = slice(j * width, (j + 1) * width)
        gz = (dot(grad_ffn, w2[cols, :], NT) * slope[:, cols].astype(f32)).astype(bf16)
        accv[8 + j] += fold(gz.astype(f32))
        acc2[cols, :] += dot(act[:, cols], grad_ffn, TN)
        acc1[:, cols] += dot(hidden_t, gz)
        grad_hidden += dot(gz, w1[:, cols], NT)
    accv[3] += fold(grad_hidden * unit_one)
    accv[4] += fold(grad_hidden)
    grad_one = norm_back(grad_hidden, unit_one, scale_one, vec_ref[3:4, :])
    gres_ref[...] = grad_one
    grad_attn = grad_one.astype(bf16)
    accv[2] += fold(grad_attn.astype(f32))
    acco[...] += dot(mixed, grad_attn, TN)
    gmixed_ref[...] = dot(grad_attn, wo[...], NT).astype(bf16)

    @pl.when(step == pl.num_programs(0) - 1)
    def _():
        gvec_ref[...] = jnp.sum(accv[...], axis=1)
        part = stage.shape[1]
        amount = mine_ref.shape[0]
        ff = chunks * width

        def send(n, side, dst, at, started):
            core = where_ref[1] if side == 0 else 1 - where_ref[1]
            row = pl.multiple_of((where_ref[2 + n] * 2 + core) * part, 8)
            rows = pl.ds(row, part)
            slot = side * SLOTS + lax.rem(n, SLOTS)
            copy = pltpu.make_async_copy(stage.at[slot], dst.at[at], out_sem.at[slot])

            @pl.when(started)
            def _():
                copy.wait()

            stage[slot, :, :ff] = acc1[rows, :].astype(bf16)
            stage[slot, :, ff : ff + width] = acco[rows, :].astype(bf16)
            for j in range(EARLY, chunks):
                spot = ff + (1 + j - EARLY) * width
                stage[slot, :, spot : spot + width] = acc2[
                    pl.ds(pl.multiple_of(j * width + row, 8), part), :
                ].astype(bf16)
            copy.start()

        depth = tall.shape[1]

        def send_down(n, _):
            slot = lax.rem(n, 4)
            copy = pltpu.make_async_copy(
                tall.at[slot], down_ref.at[pl.ds(pl.multiple_of(n * depth, depth), depth), :], tall_sem.at[slot]
            )

            @pl.when(n >= 4)
            def _():
                copy.wait()

            for j in range(EARLY):
                tall[slot, :, j * width : (j + 1) * width] = acc2[
                    pl.ds(pl.multiple_of(j * width + n * depth, depth), depth), :
                ].astype(bf16)
            copy.start()
            return 0

        lax.fori_loop(0, width // depth, send_down, 0)

        for xy, dst in ((1, theirs_1), (2, theirs_2), (3, theirs_3), (0, theirs_0)):
            lax.fori_loop(0, 4, lambda z, _: send(4 * xy + z, 1, dst, z, xy != 1) or 0, 0)
        lax.fori_loop(0, amount, lambda n, _: send(n, 0, mine_ref, n, n >= SLOTS) or 0, 0)
        for slot in range(2 * SLOTS):
            pltpu.make_async_copy(stage.at[slot], mine_ref.at[0], out_sem.at[slot]).wait()
        for slot in range(4):
            pltpu.make_async_copy(tall.at[slot], down_ref.at[pl.ds(0, depth), :], tall_sem.at[slot]).wait()


def middle(where, mixed, tokens, cotangent, vec_rows, packed, block=256):
    tok, width = tokens.shape
    chunks = (packed.shape[1] // width - 1) // 2
    chips = CHIPS
    part = width // (2 * chips)
    any_spec = pl.BlockSpec(memory_space=pl.ANY)
    row_spec = pl.BlockSpec((block, width), lambda r, *_: (r, 0))
    vec_spec = pl.BlockSpec((vec_rows.shape[0], width), lambda r, *_: (0, 0))
    ff = chunks * width
    late = ff + (1 + chunks - EARLY) * width
    return pl.pallas_call(
        middle_kernel,
        grid_spec=pltpu.PrefetchScalarGridSpec(
            num_scalar_prefetch=1,
            grid=(tok // block,),
            in_specs=[row_spec, row_spec, row_spec, vec_spec, any_spec],
            out_specs=[row_spec, row_spec, row_spec, vec_spec] + [any_spec] * 6,
            scratch_shapes=[
                pltpu.VMEM((width, ff), bf16),
                pltpu.VMEM((ff, width), bf16),
                pltpu.VMEM((width, width), bf16),
                pltpu.VMEM((width, ff), f32),
                pltpu.VMEM((ff, width), f32),
                pltpu.VMEM((width, width), f32),
                pltpu.VMEM((vec_rows.shape[0], 8, width), f32),
                pltpu.VMEM((block, ff), bf16),
                pltpu.VMEM((block, ff), bf16),
                pltpu.VMEM((2 * SLOTS, part, late), bf16),
                pltpu.VMEM((4, 64, EARLY * width), bf16),
                pltpu.SemaphoreType.DMA,
                pltpu.SemaphoreType.DMA((2 * SLOTS,)),
                pltpu.SemaphoreType.DMA((4,)),
            ],
        ),
        out_shape=[
            jax.ShapeDtypeStruct((tok, width), bf16),
            jax.ShapeDtypeStruct((tok, width), bf16),
            jax.ShapeDtypeStruct((tok, width), f32),
            jax.ShapeDtypeStruct(vec_rows.shape, f32),
            jax.ShapeDtypeStruct((width, EARLY * width), bf16),
            jax.ShapeDtypeStruct((chips, part, late), bf16),
        ]
        + [jax.ShapeDtypeStruct((4, part, late), bf16)] * 4,
        compiler_params=pltpu.CompilerParams(vmem_limit_bytes=60 * MIB),
        cost_estimate=cost(104),
        name="middle",
    )(where, mixed, tokens, cotangent, vec_rows, packed)


def attend_backward_kernel(
    where_ref, x_ref, q_ref, k_ref, v_ref, mixed_ref, gmixed_ref, probs_ref, share_ref,
    gqkv_ref, gbias_ref, mine_ref, theirs_ref,
    acc, accb, grads_scr, gscr, stage, out_sem,
):
    row = pl.program_id(0)
    length, width = q_ref.shape
    pairs = width // PAIR
    low = lax.broadcasted_iota(jnp.int32, (length, PAIR), 1) < HD
    step = 128
    reach = 256

    @pl.when(row == 0)
    def _():
        acc[...] = jnp.zeros_like(acc)
        accb[...] = jnp.zeros_like(accb)
        grads_scr[...] = jnp.zeros_like(grads_scr)

    heads = -(-width // HD // 8) * 8
    head_of = lax.broadcasted_iota(jnp.int32, (heads, width), 1) // HD
    pick_head = (head_of == lax.broadcasted_iota(jnp.int32, (heads, width), 0)).astype(bf16)
    share = jnp.concatenate([share_ref[0, p] for p in range(pairs)], axis=0)
    if heads > 2 * pairs:
        share = jnp.concatenate([share, jnp.zeros((heads - 2 * pairs, length), f32)], axis=0)
    upper = share.astype(bf16)
    lower = (share - upper.astype(f32)).astype(bf16)
    spread = dot(upper, pick_head, TN) + dot(lower, pick_head, TN)
    scaled = (gmixed_ref[...].astype(f32) * spread).astype(bf16)
    gscr[...] = scaled
    product = scaled.astype(f32) * mixed_ref[...].astype(f32)
    upper = product.astype(bf16)
    lower = (product - upper.astype(f32)).astype(bf16)
    means = dot(pick_head, upper, NT) + dot(pick_head, lower, NT)
    none = jnp.zeros((length, PAIR), bf16)

    for pair in range(pairs):
        at = slice(pair * PAIR, (pair + 1) * PAIR)
        qp, kp, vp, gp = q_ref[:, at], k_ref[:, at], v_ref[:, at], gscr[:, at]
        kt = kp.T
        for side in range(2):
            pick = low if side == 0 else jnp.logical_not(low)
            va = jnp.where(pick, vp, none)
            for b in range(length // step):
                first, last = key_span(b, step, reach, length)
                block = slice(b * step, (b + 1) * step)
                cols = slice(side * length + b * step, side * length + (b + 1) * step)
                gprobs = dot(va[first:last], gp[block], NT)
                head = 2 * pair + side
                grads = probs_ref[0, pair, first:last, cols].astype(f32) * (gprobs - means[head : head + 1, block])
                grads_scr[first:last, cols] = grads.astype(bf16)
        gq_t = jnp.concatenate(
            [dot(kt[:HD], grads_scr[:, :length]), dot(kt[HD:], grads_scr[:, length:])], axis=0
        )
        gq = (gq_t * HD**-0.5).astype(bf16).T
        both_q = jnp.concatenate([jnp.where(low, qp, none), jnp.where(low, none, qp)], axis=0)
        both_g = jnp.concatenate([jnp.where(low, gp, none), jnp.where(low, none, gp)], axis=0)
        gk = dot(grads_scr[...], both_q).astype(bf16)
        gv = dot(probs_ref[0, pair], both_g).astype(bf16)
        for s, part in enumerate((gq, gk, gv)):
            spot = slice(s * width + pair * PAIR, s * width + (pair + 1) * PAIR)
            gqkv_ref[:, spot] = part
            if s != 1:
                accb[:, spot] += fold(part.astype(f32))
    acc[...] += dot(x_ref[...], gqkv_ref[...], TN)

    @pl.when(row == pl.num_programs(0) - 1)
    def _():
        gbias_ref[...] = jnp.broadcast_to(jnp.sum(accb[...], axis=0, keepdims=True), gbias_ref.shape)
        part = stage.shape[1]
        amount = mine_ref.shape[0]

        def send(n, side, dst):
            core = where_ref[1] if side == 0 else 1 - where_ref[1]
            rows = pl.ds(pl.multiple_of((where_ref[2 + n] * 2 + core) * part, 8), part)
            slot = side * amount + n
            stage[slot] = acc[rows, :].astype(bf16)
            pltpu.make_async_copy(stage.at[slot], dst.at[n], out_sem).start()

        def body(n, _):
            send(n, 1, theirs_ref)
            send(n, 0, mine_ref)
            return 0

        lax.fori_loop(0, amount, body, 0)
        pltpu.make_async_copy(stage.at[pl.ds(0, amount)], mine_ref, out_sem).wait()
        pltpu.make_async_copy(stage.at[pl.ds(amount, amount)], theirs_ref, out_sem).wait()


def attend_backward(where, tokens, qkv, mixed, gmixed, probs, share, group, groups):
    rows = probs.shape[0]
    tok, model = tokens.shape
    length = tok // rows
    width = model // groups
    pairs = width // PAIR
    chips = CHIPS
    part = model // (2 * chips)
    any_spec = pl.BlockSpec(memory_space=pl.ANY)
    own = lambda s: pl.BlockSpec((length, width), lambda r, *_: (r, s * groups + group))
    return pl.pallas_call(
        attend_backward_kernel,
        grid_spec=pltpu.PrefetchScalarGridSpec(
            num_scalar_prefetch=1,
            grid=(rows,),
            in_specs=[
                pl.BlockSpec((length, model), lambda r, *_: (r, 0)),
                own(0), own(1), own(2), own(0), own(0),
                pl.BlockSpec((1, pairs, length, 2 * length), lambda r, *_: (r, group, 0, 0)),
                pl.BlockSpec((1, pairs, 2, length), lambda r, *_: (r, group, 0, 0)),
            ],
            out_specs=[
                pl.BlockSpec((length, 3 * width), lambda r, *_: (r, 0)),
                pl.BlockSpec((8, 3 * width), lambda r, *_: (0, 0)),
                any_spec,
                any_spec,
            ],
            scratch_shapes=[
                pltpu.VMEM((model, 3 * width), f32),
                pltpu.VMEM((8, 3 * width), f32),
                pltpu.VMEM((length, 2 * length), bf16),
                pltpu.VMEM((length, width), bf16),
                pltpu.VMEM((2 * chips, part, 3 * width), bf16),
                pltpu.SemaphoreType.DMA,
            ],
        ),
        out_shape=[
            jax.ShapeDtypeStruct((tok, 3 * width), bf16),
            jax.ShapeDtypeStruct((8, 3 * width), f32),
            jax.ShapeDtypeStruct((chips, part, 3 * width), bf16),
            jax.ShapeDtypeStruct((chips, part, 3 * width), bf16),
        ],
        compiler_params=pltpu.CompilerParams(vmem_limit_bytes=56 * MIB),
        cost_estimate=cost(57 // groups),
        name="attend_backward",
    )(where, tokens, qkv, qkv, qkv, mixed, gmixed, probs, share)


def input_grad_kernel(gres_ref, w_ref, *rest):
    parts, out_ref = rest[:-1], rest[-1]
    total = gres_ref[...]
    width = parts[0].shape[1] // 3
    for g, part in enumerate(parts):
        for s in range(3):
            total += dot(part[:, s * width : (s + 1) * width], w_ref[s, :, g * width : (g + 1) * width], NT)
    out_ref[...] = total.astype(bf16)


def input_grad(gres, weights, parts, block=512):
    tok, model = gres.shape
    return pl.pallas_call(
        input_grad_kernel,
        grid=(tok // block,),
        in_specs=[
            pl.BlockSpec((block, model), lambda r: (r, 0)),
            pl.BlockSpec(weights.shape, lambda r: (0, 0, 0)),
        ]
        + [pl.BlockSpec((block, p.shape[1]), lambda r: (r, 0)) for p in parts],
        out_specs=pl.BlockSpec((block, model), lambda r: (r, 0)),
        out_shape=jax.ShapeDtypeStruct((tok, model), bf16),
        compiler_params=pltpu.CompilerParams(vmem_limit_bytes=56 * MIB),
        cost_estimate=cost(0.1),
        name="input_grad",
    )(gres, weights, *parts)


beta_one = 0.5
beta_two = 0.5
adam_eps = 1e-06
decay_rate = 0.01
learn_rate = 0.3
ema_rate = 0.5
ratio_eps = 1e-06
STEP = 7


def whole_sum(v):
    return jnp.sum(jnp.sum(v, axis=0, keepdims=True), axis=1, keepdims=True)


def spread_vec(vec, part):
    return jnp.concatenate([vec[:, c * 128 : (c + 1) * 128] for c in range(vec.shape[1] // 128)], axis=0)


def joined_vec(rows):
    return jnp.concatenate([rows[16 * c : 16 * c + 16] for c in range(rows.shape[0] // 16)], axis=1)


def near_kernel(mine_ref, came_ref, vec_ref, vec_came_ref, *sent_refs):
    part, width = mine_ref.shape[1:]
    vec = spread_vec(vec_ref[...] + vec_came_ref[...], part)
    for xy in range(3):
        for z in range(4):
            at = 4 * xy + 4 + z
            sent_refs[xy][z, :, :width] = (mine_ref[at].astype(f32) + came_ref[at].astype(f32)).astype(bf16)
            sent_refs[xy][z, :, width:] = vec[z * part : (z + 1) * part].astype(bf16)


def near(mine, came, vec, vec_came):
    chips, part, width = mine.shape
    return pl.pallas_call(
        near_kernel,
        out_shape=[jax.ShapeDtypeStruct((4, part, width + 128), bf16)] * 3,
        compiler_params=pltpu.CompilerParams(vmem_limit_bytes=56 * MIB),
        cost_estimate=cost(0.1),
        name="near",
    )(mine, came, vec, vec_came)


def line_kernel(with_vec, *refs):
    mine_ref, came_ref = refs[:2]
    parts = refs[2:5]
    refs = refs[5:]
    if with_vec:
        vec_ref, vec_came_ref = refs[:2]
        refs = refs[2:]
    part, width = mine_ref.shape[1:]
    if with_vec:
        vec = spread_vec(vec_ref[...] + vec_came_ref[...], part)
        blocks = []
        for z in range(4):
            block = vec[z * part : (z + 1) * part]
            for p in parts:
                block = block + p[z, :, width:].astype(f32)
            blocks.append(block)
        low = jnp.concatenate(blocks, axis=1).astype(bf16)
        refs[4][...] = joined_vec(jnp.concatenate(blocks, axis=0))
    for z in range(4):
        rows = mine_ref[z].astype(f32) + came_ref[z].astype(f32)
        for p in parts:
            rows = rows + p[z, :, :width].astype(f32)
        if z == 0:
            refs[0][...] = rows
        else:
            refs[z][:, :width] = rows.astype(bf16)
            if with_vec:
                refs[z][:, width:] = low


def line(mine, came, parts, vecs=()):
    chips, part, width = mine.shape
    wide = width + (512 if vecs else 0)
    full = lambda a: pl.BlockSpec(a.shape, lambda i: (0,) * a.ndim)
    first = pl.BlockSpec((4, part, width), lambda i: (0, 0, 0))
    shapes = [jax.ShapeDtypeStruct((part, width), f32)] + [jax.ShapeDtypeStruct((part, wide), bf16)] * 3
    if vecs:
        shapes.append(jax.ShapeDtypeStruct(vecs[0].shape, f32))
    return pl.pallas_call(
        functools.partial(line_kernel, bool(vecs)),
        grid=(1,),
        in_specs=[first, first] + [full(p) for p in parts] + [full(v) for v in vecs],
        out_specs=[full(o) for o in shapes],
        out_shape=shapes,
        compiler_params=pltpu.CompilerParams(vmem_limit_bytes=56 * MIB),
        cost_estimate=cost(0.1),
        name="line",
    )(mine, came, *parts, *vecs)


def own_grads_kernel(amount, where_ref, rows_ref, vec_ref, *refs):
    parts = refs[:amount]
    gq_ref, gv_ref, gb_ref = refs[amount:]
    part, width = rows_ref.shape
    model = width // 3
    rows = rows_ref[...]
    for p in parts:
        rows = rows + p[:, :width].astype(f32)
    for s in range(3):
        gq_ref[s] = rows[:, s * model : (s + 1) * model]
    vec = vec_ref[...]
    if amount:
        blocks = []
        for z in range(4):
            block = jnp.zeros((part, 128), f32)
            for p in parts:
                block = block + p[:, width + z * 128 : width + (z + 1) * 128].astype(f32)
            blocks.append(block)
        vec = vec + joined_vec(jnp.concatenate(blocks, axis=0))
    first = where_ref[0] * part
    chunks = gb_ref.shape[1] // part

    def picked(values, count, repeat):
        place = lax.broadcasted_iota(jnp.int32, (model, count), 0)
        wanted = first + lax.broadcasted_iota(jnp.int32, (model, count), 1) // repeat
        pick = jnp.where(place == wanted, 1.0, 0.0)
        return lax.dot_general(values, pick, NN, precision=lax.Precision.HIGHEST, preferred_element_type=f32)

    gv_ref[...] = picked(vec[0:8], part, 1)
    spread = picked(vec[8:16], chunks * part, chunks)
    row = lax.broadcasted_iota(jnp.int32, spread.shape, 0)
    lane = lax.broadcasted_iota(jnp.int32, spread.shape, 1)
    gb_ref[...] = jnp.sum(jnp.where(lane % chunks == row, spread, 0.0), axis=0, keepdims=True)


def own_grads(index, rows, vec, parts, chunks):
    part, width = rows.shape
    model = width // 3
    spec = pl.BlockSpec(memory_space=pltpu.VMEM)
    return pl.pallas_call(
        functools.partial(own_grads_kernel, len(parts)),
        in_specs=[pl.BlockSpec(memory_space=pltpu.SMEM)] + [spec] * (2 + len(parts)),
        out_specs=[spec] * 3,
        out_shape=[
            jax.ShapeDtypeStruct((3, part, model), f32),
            jax.ShapeDtypeStruct((8, part), f32),
            jax.ShapeDtypeStruct((1, chunks * part), f32),
        ],
        compiler_params=pltpu.CompilerParams(vmem_limit_bytes=56 * MIB),
        cost_estimate=cost(0.1),
        name="own_grads",
    )(index, rows, vec, *parts)


def moments_kernel(kinds, *refs):
    n = len(kinds)
    grads, masters, firsts, seconds = (refs[i * n : (i + 1) * n] for i in range(4))
    new_firsts, new_seconds, updates = (refs[(4 + i) * n : (5 + i) * n] for i in range(3))
    squares_ref = refs[7 * n]
    lane = lax.broadcasted_iota(jnp.int32, squares_ref.shape, 1)
    row = lax.broadcasted_iota(jnp.int32, squares_ref.shape, 0)
    squares = jnp.zeros(squares_ref.shape, f32)
    corr_one = 1.0 - beta_one**STEP
    corr_two = 1.0 - beta_two**STEP
    for i, (spot, amount) in enumerate(kinds):
        grad = grads[i][...]
        master = masters[i][...]
        first = beta_one * firsts[i][...] + (1.0 - beta_one) * grad
        second = beta_two * seconds[i][...] + (1.0 - beta_two) * grad * grad
        update = first / corr_one / (jnp.sqrt(second / corr_two) + adam_eps) + decay_rate * master
        new_firsts[i][...] = first
        new_seconds[i][...] = second
        updates[i][...] = update
        for k in range(amount):
            if amount == 1:
                pair = (master, update)
            elif len(master.shape) == 3:
                pair = (master[k], update[k])
            else:
                pair = (master[k : k + 1], update[k : k + 1])
            for r, v in enumerate(pair):
                squares = jnp.where((lane == spot + k) & (row == r), whole_sum(v * v), squares)
    squares_ref[...] = squares


def moments(kinds, grads, masters, firsts, seconds):
    shapes = [jax.ShapeDtypeStruct(m.shape, f32) for m in masters]
    n = len(kinds)
    out = pl.pallas_call(
        functools.partial(moments_kernel, kinds),
        out_shape=shapes * 3 + [jax.ShapeDtypeStruct((8, 128), f32)],
        compiler_params=pltpu.CompilerParams(vmem_limit_bytes=56 * MIB),
        cost_estimate=cost(0.1),
        name="moments",
    )(*grads, *masters, *firsts, *seconds)
    return out[:n], out[n : 2 * n], out[2 * n : 3 * n], out[3 * n]


def renew_kernel(kinds, came_ref, *refs):
    n = len(kinds)
    masters, updates, averages = (refs[i * n : (i + 1) * n] for i in range(3))
    news, emas, copies = (refs[(3 + i) * n : (4 + i) * n] for i in range(3))
    norm_ref, ratio_ref = refs[6 * n :]
    total = jnp.sum(came_ref[...], axis=0)
    norms = jnp.sqrt(total)
    ratios = norms[0:1] / jnp.sqrt(total[1:2] + ratio_eps)
    norm_ref[...] = norms[0:2, : norm_ref.shape[1]]
    ratio_ref[...] = ratios[:, : ratio_ref.shape[1]]
    lane = lax.broadcasted_iota(jnp.int32, ratios.shape, 1)
    for i, (spot, amount) in enumerate(kinds):
        for k in range(amount):
            at = ... if amount == 1 else (k if len(masters[i].shape) == 3 else slice(k, k + 1))
            ratio = jnp.sum(jnp.where(lane == spot + k, ratios, 0.0), axis=1, keepdims=True)
            new = masters[i][at] - learn_rate * ratio * updates[i][at]
            news[i][at] = new
            emas[i][at] = ema_rate * averages[i][at] + (1.0 - ema_rate) * new
            copies[i][at] = new.astype(bf16)


def renew(kinds, came, masters, updates, averages):
    shapes = [jax.ShapeDtypeStruct(m.shape, f32) for m in masters]
    halves = [jax.ShapeDtypeStruct(m.shape, bf16) for m in masters]
    n = len(kinds)
    out = pl.pallas_call(
        functools.partial(renew_kernel, kinds),
        out_shape=shapes * 2 + halves + [jax.ShapeDtypeStruct((2, 15), f32), jax.ShapeDtypeStruct((1, 15), f32)],
        compiler_params=pltpu.CompilerParams(vmem_limit_bytes=56 * MIB),
        cost_estimate=cost(0.1),
        name="renew",
    )(came, *masters, *updates, *averages)
    return out[:n], out[n : 2 * n], out[2 * n : 3 * n], out[3 * n], out[3 * n + 1].reshape(15)


class Ring:
    def __init__(self, sizes):
        self.sizes = sizes
        self.amount = sizes["gx"] * sizes["gy"]
        self.near = sizes == {"gx": 8, "gy": 4}

    def index(self):
        return lax.axis_index("gx") * self.sizes["gy"] + lax.axis_index("gy")

    def swap(self, value, bits):
        return lax.ppermute(value, ALL, [(i, i ^ bits) for i in range(self.amount)])

    def core(self, value):
        return self.swap(value, 1)

    def plane(self, value, k):
        return self.swap(value, k << 1)

    def line(self, value, k):
        return self.swap(value, k << 3)


def where_am_i(ring):
    if not ring.near:
        return jnp.asarray([0, 0] + list(range(CHIPS)), jnp.int32)
    me = ring.index()
    chip = me // 2
    order = [chip ^ ((z << 2) | xy) for xy in range(4) for z in range(4)]
    return jnp.stack([chip, me % 2] + order).astype(jnp.int32)


def gather_first(ring, w_qkv, vec_part):
    low = w_qkv.astype(bf16)
    part, width = low.shape[1], low.shape[2]
    half = width // 2
    vec_rows = vec_part.shape[0]
    vec_part = vec_part.astype(bf16)
    if not ring.near:
        full = lax.all_gather(low, ALL, axis=1, tiled=True)
        blocks = full.reshape(3, CHIPS, width // CHIPS, 2, half).transpose(3, 1, 0, 2, 4)
        blocks = blocks.reshape(8, 4 * 3 * width // CHIPS, half)
        vecs = lax.all_gather(vec_part, ALL, axis=1, tiled=True)
        return [blocks[i] for i in range(8)], vecs.astype(f32)
    me = ring.index()
    core = me % 2
    spread = jnp.zeros((16, width), bf16)
    spread = lax.dynamic_update_slice(spread, vec_part, (0, me * part))
    spread = spread.reshape(32, half)
    left, right = low[:, :, :half], low[:, :, half:]
    keep = jnp.where(core == 0, left, right)
    give = jnp.where(core == 0, right, left)
    got = ring.core(jnp.concatenate([give.reshape(3 * part, half), spread], axis=0))
    came = got[: 3 * part].reshape(3, part, half)
    block = jnp.where(
        core == 0, jnp.concatenate([keep, came], axis=1), jnp.concatenate([came, keep], axis=1)
    ).reshape(6 * part, half)
    payload = jnp.concatenate([block, spread + got[3 * part :]], axis=0)
    cut = 6 * part
    lines = [payload] + [ring.line(payload, k) for k in (1, 2, 3)]
    total = lines[0][cut:] + lines[1][cut:] + lines[2][cut:] + lines[3][cut:]
    payload = jnp.concatenate([v[:cut] for v in lines] + [total], axis=0)
    mine = [payload] + [ring.plane(payload, k) for k in (1, 2, 3)]
    theirs = [ring.core(v) for v in mine]
    cut = 4 * cut
    total = mine[0][cut:] + mine[1][cut:] + mine[2][cut:] + mine[3][cut:]
    return mine + theirs, total.reshape(16, width)[:vec_rows].astype(f32)


def gather_rest(w_out, w_up, w_down):
    part, width = w_out.shape
    chunks = w_up.shape[1] // width
    up = w_up.astype(bf16).reshape(part, width, chunks).transpose(0, 2, 1).reshape(part, chunks * width)
    down = w_down.astype(bf16).reshape(part, chunks * width)
    packed = jnp.concatenate([up, down, w_out.astype(bf16)], axis=1)
    return lax.all_gather(packed, ALL, axis=0, tiled=True)


def after(value, *others):
    return lax.optimization_barrier((value,) + others)[0]


def scatter_far(mine, theirs):
    chips, part, width = mine.shape
    full = jnp.stack([mine, theirs], axis=1).reshape(2 * chips * part, width)
    return lax.psum_scatter(full, ALL, scatter_dimension=0, tiled=True).astype(f32)


def share(ring, squares):
    if not ring.near:
        return lax.psum(squares, ALL)[None]
    return lax.all_to_all(jnp.broadcast_to(squares[None], (ring.amount,) + squares.shape), ALL, 0, 0)


def on_device(
    ring,
    tokens,
    seg_lengths,
    cotangent,
    *params,
):
    masters = params[0:6]
    averages = params[18:24]
    w_qkv, w_out, w_up, w_down, vecs, b_up = masters
    part, width = w_out.shape
    chunks = w_up.shape[1] // width
    bounds = jnp.stack(
        [jnp.sum(seg_lengths[:, : k + 1], axis=1) for k in range(seg_lengths.shape[1])], axis=1
    ).astype(jnp.int32)
    where = where_am_i(ring)
    packed = gather_rest(w_out, w_up, w_down)
    vec_part = jnp.concatenate([vecs, b_up.reshape(part, chunks).T], axis=0)
    raws, vec_rows = gather_first(ring, w_qkv, vec_part)
    vec_rows = jnp.concatenate([vec_rows, jnp.zeros((4, width), f32)], axis=0)
    qkv, mixed, probs, share_rows, full_qkv = attend_forward(where, bounds, tokens, vec_rows, raws)
    layer_out, gmixed, gres, gvec, down, mine, *theirs = middle(
        where, mixed, tokens, cotangent, vec_rows, packed
    )
    down = lax.psum_scatter(down, ALL, scatter_dimension=0, tiled=True)
    firsts_in = list(params[6:12])
    seconds_in = list(params[12:18])

    def join_vec(gvec, gbias):
        gbias = gbias[0].reshape(3, width)
        return jnp.concatenate([gbias[0:1], gbias[2:3], gvec[2:]], axis=0)

    if ring.near:
        came = [None] * 4
        for k in (1, 2, 3, 0):
            came[k] = ring.core(theirs[k])
        sent = [
            (mine[4 * k : 4 * k + 4].astype(f32) + came[k].astype(f32)).astype(bf16) for k in (1, 2, 3)
        ]
        parts = [ring.plane(v, k + 1) for k, v in enumerate(sent)]
        gate = after(gmixed, came[0], *sent)
        gqkv, gbias, mine_q, theirs_q = attend_backward(where, tokens, qkv, mixed, gate, probs, share_rows, 0, 1)
        gvec = join_vec(gvec, after(gbias, *parts))
        came_q = ring.core(after(theirs_q, *parts))
        vec_came = ring.core(gvec)
        sent_q = near(mine_q, came_q, gvec, vec_came)
        parts_q = [ring.plane(v, k + 1) for k, v in enumerate(sent_q)]
        parts[0] = after(parts[0], *sent_q)
        rows, *sent = line(mine, came[0], parts)
        grad_input = input_grad(after(gres, *sent, *sent_q), full_qkv, [gqkv])
        sent[2] = after(sent[2], grad_input)
        parts = [ring.line(v, k + 1) for k, v in enumerate(sent)]
        parts_q[0] = after(parts_q[0], grad_input, parts[0], parts[1])
        rows_q, *sent_q, vec_q = line(mine_q, came_q, parts_q, (gvec, vec_came))
        parts_q = [ring.line(v, k + 1) for k, v in enumerate(sent_q)]
        rows = after(rows, *sent_q)
        down = after(down, *sent_q)
        grad_rest = rows + parts[0].astype(f32) + parts[1].astype(f32) + parts[2].astype(f32)
    else:
        gqkv, gbias, mine_q, theirs_q = attend_backward(where, tokens, qkv, mixed, gmixed, probs, share_rows, 0, 1)
        grad_input = input_grad(gres, full_qkv, [gqkv])
        grad_rest = scatter_far(mine, jnp.concatenate(theirs, axis=0))
        rows_q, vec_q, parts_q = scatter_far(mine_q, theirs_q), lax.psum(join_vec(gvec, gbias), ALL), []
    ff = chunks * width
    kinds = ((3, 1), (4, 1), (5, 1))
    grad_down = jnp.concatenate([down.astype(f32), grad_rest[:, ff + width :]], axis=1)
    grads = (
        grad_rest[:, ff : ff + width],
        grad_rest[:, :ff].reshape(part, chunks, width).transpose(0, 2, 1).reshape(part, ff),
        grad_down.reshape(part * chunks, width),
    )
    firsts_r, seconds_r, updates_r, squares_r = moments(
        kinds, grads, masters[1:4], firsts_in[1:4], seconds_in[1:4]
    )
    if parts_q:
        parts_q[0] = after(parts_q[0], squares_r)
    index = ring.index().reshape(1).astype(jnp.int32)
    grads = own_grads(index, rows_q, vec_q, parts_q, chunks)
    flat = lambda v: v.reshape(1, -1)
    pick = lambda v: (v[0], v[4], flat(v[5]))
    others = ((0, 3), (6, 8), (14, 1))
    firsts_q, seconds_q, updates_q, squares_q = moments(
        others, grads, pick(masters), pick(firsts_in), pick(seconds_in)
    )
    came = share(ring, squares_r + squares_q)
    news, emas, copies, norms, ratios = renew(
        kinds + others,
        came,
        tuple(masters[1:4]) + pick(masters),
        tuple(updates_r) + tuple(updates_q),
        tuple(averages[1:4]) + pick(averages),
    )
    order = lambda v: (v[3], v[0], v[1], v[2], v[4], v[5].reshape(-1))
    out = [layer_out, grad_input]
    for found in (news, list(firsts_r) + list(firsts_q), list(seconds_r) + list(seconds_q), emas, copies):
        out.extend(order(found))
    return (*out, ratios, norms)


def solution(mesh):
    ring = Ring(dict(mesh.shape))
    rows = P(ALL, None)
    kinds = (P(None, ALL, None), rows, rows, rows, P(None, ALL), P(ALL))
    return jax.shard_map(
        functools.partial(on_device, ring),
        mesh=mesh,
        in_specs=(rows, rows, rows) + kinds * 4,
        out_specs=(rows, rows) + kinds * 5 + (P(), P()),
        check_vma=False,
    )
```

```python
import functools

import jax
import jax.numpy as jnp
from jax import lax
from jax.experimental import pallas as pl
from jax.experimental.pallas import tpu as pltpu
from jax.sharding import PartitionSpec as P

ALL = ("gx", "gy")

HEADS = 12
HD = 64
PAIR = 2 * HD
MASKED = -1e30
CHIPS = 16
MIB = 1 << 20
f32 = jnp.float32
bf16 = jnp.bfloat16
NT = (((1,), (1,)), ((), ()))
NN = (((1,), (0,)), ((), ()))
TN = (((0,), (0,)), ((), ()))


def dot(a, b, dims=NN):
    return lax.dot_general(a, b, dims, preferred_element_type=f32)


def cost(us):
    return pl.CostEstimate(flops=int(us * 1.1e9), bytes_accessed=int(us * 1e6), transcendentals=0)


def seg_of(bounds_ref, row, shape, dim):
    place = lax.broadcasted_iota(jnp.int32, shape, dim)
    total = jnp.zeros(shape, jnp.int32)
    for k in range(bounds_ref.shape[1]):
        total += (place >= bounds_ref[row, k]).astype(jnp.int32)
    return total


def seg_columns(bounds_ref, row, length):
    shape = (length, PAIR)
    seg = seg_of(bounds_ref, row, shape, 0)
    lane = lax.broadcasted_iota(jnp.int32, shape, 1)
    low = lane < HD
    spot = jnp.where(low, lane, lane - HD)
    same = spot == seg
    inside = spot < 4
    query_cols = jnp.where(same, 1.0, 0.0).astype(bf16)
    key_cols = jnp.where(inside, jnp.where(same, 0.0, MASKED), 0.0).astype(bf16)
    return low, query_cols, key_cols


def load_qkv(where_ref, raws, w_scr, sem):
    chip, core = where_ref[0], where_ref[1]
    half = w_scr.shape[2] // 2
    copies = []
    for side in range(2):
        col = pl.multiple_of((core if side == 0 else 1 - core) * half, PAIR)
        for xy in range(4):
            raw = raws[side * 4 + xy]
            for z in range(4):
                at = where_ref[2 + xy * 4 + z]
                rows = w_scr.shape[1] // CHIPS
                for s in range(3):
                    copies.append(
                        pltpu.make_async_copy(
                            raw.at[pl.ds((3 * z + s) * rows, rows), :],
                            w_scr.at[s, pl.ds(pl.multiple_of(at * rows, 16), rows), pl.ds(col, half)],
                            sem,
                        )
                    )
    for c in copies:
        c.start()
    for c in copies:
        c.wait()


def key_span(block, step, reach, length):
    first = max(0, block * step - (reach - 1)) // step * step
    last = min(length, -(-((block + 1) * step - 1 + reach) // step) * step)
    return first, last


def attend_forward_kernel(
    where_ref, bounds_ref, x_ref, vec_ref, *rest
):
    raws = rest[:8]
    qkv_ref, o_ref, probs_ref, share_ref, wout_ref, w_scr, qkv_scr, sem, out_sem = rest[8:]
    row = pl.program_id(0)
    length = x_ref.shape[0]
    width = x_ref.shape[1]

    @pl.when(row == 0)
    def _():
        load_qkv(where_ref, raws, w_scr, sem)
        pltpu.make_async_copy(w_scr, wout_ref, out_sem).start()

    x = x_ref[...]
    q = (dot(x, w_scr[0]) + vec_ref[0:1, :]).astype(bf16) * jnp.asarray(HD**-0.5, bf16)
    qkv_scr[:, 0:width] = q
    qkv_scr[:, width : 2 * width] = dot(x, w_scr[1]).astype(bf16)
    qkv_scr[:, 2 * width : 3 * width] = (dot(x, w_scr[2]) + vec_ref[1:2, :]).astype(bf16)
    qkv_ref[...] = qkv_scr[...]
    low, query_cols, key_cols = seg_columns(bounds_ref, row, length)
    sub = lax.broadcasted_iota(jnp.int32, (PAIR, length), 0)
    step = 128
    reach = 256

    def pair_body(pair, _):
        at = pl.multiple_of(pair * PAIR, PAIR)
        qp = qkv_scr[:, pl.ds(at, PAIR)]
        kp = qkv_scr[:, pl.ds(width + at, PAIR)]
        vt = qkv_scr[:, pl.ds(2 * width + at, PAIR)].T
        outs = []
        tops = []
        for side in range(2):
            pick = low if side == 0 else jnp.logical_not(low)
            qa = jnp.where(pick, qp, query_cols)
            ka = jnp.where(pick, kp, key_cols)
            if side == 0:
                va = jnp.where(sub < HD, vt, (sub == HD).astype(bf16))
            else:
                va = jnp.where(sub < HD, (sub == 0).astype(bf16), vt)
            blocks = []
            shares = []
            for b in range(length // step):
                first, last = key_span(b, step, reach, length)
                scores = dot(ka[first:last], qa[b * step : (b + 1) * step], NT)
                peak = jnp.max(scores, axis=0, keepdims=True)
                probs = jnp.exp(scores - peak).astype(bf16)
                cols = slice(side * length + b * step, side * length + (b + 1) * step)
                probs_ref[0, pair, first:last, cols] = probs
                if first > 0:
                    probs_ref[0, pair, 0:first, cols] = jnp.zeros((first, step), bf16)
                if last < length:
                    probs_ref[0, pair, last:length, cols] = jnp.zeros((length - last, step), bf16)
                mixed = dot(va[:, first:last], probs)
                total = mixed[HD : HD + 1] if side == 0 else mixed[0:1]
                mine = mixed[:HD] if side == 0 else mixed[HD:]
                share = 1.0 / total
                blocks.append((mine * share).astype(bf16))
                shares.append(share)
            outs.append(jnp.concatenate(blocks, axis=1))
            tops.append(jnp.concatenate(shares, axis=1))
        o_ref[:, pl.ds(at, PAIR)] = jnp.concatenate(outs, axis=0).T
        share_ref[0, pl.ds(pair, 1)] = jnp.concatenate(tops, axis=0)[None]
        return 0

    lax.fori_loop(0, width // PAIR, pair_body, 0, unroll=True)

    @pl.when(row == pl.num_programs(0) - 1)
    def _():
        pltpu.make_async_copy(w_scr, wout_ref, out_sem).wait()


def attend_forward(where, bounds, tokens, vec_rows, raws):
    rows = bounds.shape[0]
    tok, width = tokens.shape
    length = tok // rows
    pairs = width // PAIR
    any_spec = pl.BlockSpec(memory_space=pl.ANY)
    return pl.pallas_call(
        attend_forward_kernel,
        grid_spec=pltpu.PrefetchScalarGridSpec(
            num_scalar_prefetch=2,
            grid=(rows,),
            in_specs=[
                pl.BlockSpec((length, width), lambda r, *_: (r, 0)),
                pl.BlockSpec(vec_rows.shape, lambda r, *_: (0, 0)),
            ]
            + [any_spec] * 8,
            out_specs=[
                pl.BlockSpec((length, 3 * width), lambda r, *_: (r, 0)),
                pl.BlockSpec((length, width), lambda r, *_: (r, 0)),
                pl.BlockSpec((1, pairs, length, 2 * length), lambda r, *_: (r, 0, 0, 0)),
                pl.BlockSpec((1, pairs, 2, length), lambda r, *_: (r, 0, 0, 0)),
                any_spec,
            ],
            scratch_shapes=[
                pltpu.VMEM((3, width, width), bf16),
                pltpu.VMEM((length, 3 * width), bf16),
                pltpu.SemaphoreType.DMA,
                pltpu.SemaphoreType.DMA,
            ],
        ),
        out_shape=[
            jax.ShapeDtypeStruct((tok, 3 * width), bf16),
            jax.ShapeDtypeStruct((tok, width), bf16),
            jax.ShapeDtypeStruct((rows, pairs, length, 2 * length), bf16),
            jax.ShapeDtypeStruct((rows, pairs, 2, length), f32),
            jax.ShapeDtypeStruct((3, width, width), bf16),
        ],
        compiler_params=pltpu.CompilerParams(vmem_limit_bytes=56 * MIB),
        cost_estimate=cost(30),
        name="attend_forward",
    )(where, bounds, tokens, vec_rows, *raws)


def lane_mean(v):
    return jnp.mean(v, axis=1, keepdims=True)


def norm_parts(v):
    center = v - lane_mean(v)
    scale = lax.rsqrt(lane_mean(center * center) + 1e-12)
    return center * scale, scale


def norm_back(grad, unit, scale, gain):
    grad_unit = grad * gain
    return scale * (grad_unit - lane_mean(grad_unit) - unit * lane_mean(grad_unit * unit))


def fold(v):
    return jnp.sum(v.reshape(v.shape[0] // 8, 8, v.shape[1]), axis=0)


def gelu_both(z):
    size = jnp.abs(z)
    t = pl.reciprocal(1.0 + (0.3275911 * 0.5**0.5) * size, approx=False)
    e = jnp.exp(-0.5 * z * z)
    poly = 0.5 * 1.061405429
    for a in (-1.453152027, 1.421413741, -0.284496736, 0.254829592):
        poly = poly * t + 0.5 * a
    tail = poly * t * e
    cdf = jnp.where(z >= 0, 1.0 - tail, tail)
    return z * cdf, cdf + z * e * 0.3989422804014327


SLOTS = 4
EARLY = 3


def middle_kernel(
    where_ref, mixed_ref, x_ref, cot_ref, vec_ref, packed_ref,
    out_ref, gmixed_ref, gres_ref, gvec_ref, down_ref, mine_ref, theirs_0, theirs_1, theirs_2, theirs_3,
    w1, w2, wo, acc1, acc2, acco, accv, act, slope, stage, tall, in_sem, out_sem, tall_sem,
):
    step = pl.program_id(0)
    width = x_ref.shape[1]
    chunks = w1.shape[1] // width

    @pl.when(step == 0)
    def _():
        copies = [pltpu.make_async_copy(packed_ref.at[:, pl.ds(2 * chunks * width, width)], wo, in_sem)]
        copies.append(pltpu.make_async_copy(packed_ref.at[:, pl.ds(0, chunks * width)], w1, in_sem))
        for j in range(chunks):
            copies.append(
                pltpu.make_async_copy(
                    packed_ref.at[:, pl.ds((chunks + j) * width, width)], w2.at[pl.ds(j * width, width), :], in_sem
                )
            )
        for c in copies:
            c.start()
        acc1[...] = jnp.zeros_like(acc1)
        acc2[...] = jnp.zeros_like(acc2)
        acco[...] = jnp.zeros_like(acco)
        accv[...] = jnp.zeros_like(accv)
        for c in copies:
            c.wait()

    mixed = mixed_ref[...]
    res_one = x_ref[...].astype(f32) + dot(mixed, wo[...]) + vec_ref[2:3, :]
    unit_one, scale_one = norm_parts(res_one)
    hidden = unit_one * vec_ref[3:4, :] + vec_ref[4:5, :]
    hidden_low = hidden.astype(bf16)
    ffn = hidden + vec_ref[5:6, :]
    z = dot(hidden_low, w1[:, 0:width]) + vec_ref[8:9, :]
    for j in range(chunks):
        cols = slice(j * width, (j + 1) * width)
        if j + 1 < chunks:
            z_next = dot(hidden_low, w1[:, (j + 1) * width : (j + 2) * width]) + vec_ref[9 + j : 10 + j, :]
        g, d = gelu_both(z)
        g = g.astype(bf16)
        act[:, cols] = g
        slope[:, cols] = d.astype(slope.dtype)
        ffn += dot(g, w2[cols, :])
        z = z_next
    unit_two, scale_two = norm_parts(ffn)
    out_ref[...] = (unit_two * vec_ref[6:7, :] + vec_ref[7:8, :]).astype(bf16)
    grad = cot_ref[...].astype(f32)
    accv[6] += fold(grad * unit_two)
    accv[7] += fold(grad)
    grad_two = norm_back(grad, unit_two, scale_two, vec_ref[6:7, :])
    grad_ffn = grad_two.astype(bf16)
    accv[5] += fold(grad_ffn.astype(f32))
    grad_hidden = grad_two
    hidden_t = hidden_low.T
    for j in range(chunks):
        cols = slice(j * width, (j + 1) * width)
        gz = (dot(grad_ffn, w2[cols, :], NT) * slope[:, cols].astype(f32)).astype(bf16)
        accv[8 + j] += fold(gz.astype(f32))
        acc2[cols, :] += dot(act[:, cols], grad_ffn, TN)
        acc1[:, cols] += dot(hidden_t, gz)
        grad_hidden += dot(gz, w1[:, cols], NT)
    accv[3] += fold(grad_hidden * unit_one)
    accv[4] += fold(grad_hidden)
    grad_one = norm_back(grad_hidden, unit_one, scale_one, vec_ref[3:4, :])
    gres_ref[...] = grad_one
    grad_attn = grad_one.astype(bf16)
    accv[2] += fold(grad_attn.astype(f32))
    acco[...] += dot(mixed, grad_attn, TN)
    gmixed_ref[...] = dot(grad_attn, wo[...], NT).astype(bf16)

    @pl.when(step == pl.num_programs(0) - 1)
    def _():
        gvec_ref[...] = jnp.sum(accv[...], axis=1)
        part = stage.shape[1]
        amount = mine_ref.shape[0]
        ff = chunks * width

        def send(n, side, dst, at, started):
            core = where_ref[1] if side == 0 else 1 - where_ref[1]
            row = pl.multiple_of((where_ref[2 + n] * 2 + core) * part, 8)
            rows = pl.ds(row, part)
            slot = side * SLOTS + lax.rem(n, SLOTS)
            copy = pltpu.make_async_copy(stage.at[slot], dst.at[at], out_sem.at[slot])

            @pl.when(started)
            def _():
                copy.wait()

            stage[slot, :, :ff] = acc1[rows, :].astype(bf16)
            stage[slot, :, ff : ff + width] = acco[rows, :].astype(bf16)
            for j in range(EARLY, chunks):
                spot = ff + (1 + j - EARLY) * width
                stage[slot, :, spot : spot + width] = acc2[
                    pl.ds(pl.multiple_of(j * width + row, 8), part), :
                ].astype(bf16)
            copy.start()

        depth = tall.shape[1]

        def send_down(n, _):
            slot = lax.rem(n, 4)
            copy = pltpu.make_async_copy(
                tall.at[slot], down_ref.at[pl.ds(pl.multiple_of(n * depth, depth), depth), :], tall_sem.at[slot]
            )

            @pl.when(n >= 4)
            def _():
                copy.wait()

            for j in range(EARLY):
                tall[slot, :, j * width : (j + 1) * width] = acc2[
                    pl.ds(pl.multiple_of(j * width + n * depth, depth), depth), :
                ].astype(bf16)
            copy.start()
            return 0

        lax.fori_loop(0, width // depth, send_down, 0)

        for xy, dst in ((1, theirs_1), (2, theirs_2), (3, theirs_3), (0, theirs_0)):
            lax.fori_loop(0, 4, lambda z, _: send(4 * xy + z, 1, dst, z, xy != 1) or 0, 0)
        lax.fori_loop(0, amount, lambda n, _: send(n, 0, mine_ref, n, n >= SLOTS) or 0, 0)
        for slot in range(2 * SLOTS):
            pltpu.make_async_copy(stage.at[slot], mine_ref.at[0], out_sem.at[slot]).wait()
        for slot in range(4):
            pltpu.make_async_copy(tall.at[slot], down_ref.at[pl.ds(0, depth), :], tall_sem.at[slot]).wait()


def middle(where, mixed, tokens, cotangent, vec_rows, packed, block=256):
    tok, width = tokens.shape
    chunks = (packed.shape[1] // width - 1) // 2
    chips = CHIPS
    part = width // (2 * chips)
    any_spec = pl.BlockSpec(memory_space=pl.ANY)
    row_spec = pl.BlockSpec((block, width), lambda r, *_: (r, 0))
    vec_spec = pl.BlockSpec((vec_rows.shape[0], width), lambda r, *_: (0, 0))
    ff = chunks * width
    late = ff + (1 + chunks - EARLY) * width
    return pl.pallas_call(
        middle_kernel,
        grid_spec=pltpu.PrefetchScalarGridSpec(
            num_scalar_prefetch=1,
            grid=(tok // block,),
            in_specs=[row_spec, row_spec, row_spec, vec_spec, any_spec],
            out_specs=[row_spec, row_spec, row_spec, vec_spec] + [any_spec] * 6,
            scratch_shapes=[
                pltpu.VMEM((width, ff), bf16),
                pltpu.VMEM((ff, width), bf16),
                pltpu.VMEM((width, width), bf16),
                pltpu.VMEM((width, ff), f32),
                pltpu.VMEM((ff, width), f32),
                pltpu.VMEM((width, width), f32),
                pltpu.VMEM((vec_rows.shape[0], 8, width), f32),
                pltpu.VMEM((block, ff), bf16),
                pltpu.VMEM((block, ff), bf16),
                pltpu.VMEM((2 * SLOTS, part, late), bf16),
                pltpu.VMEM((4, 64, EARLY * width), bf16),
                pltpu.SemaphoreType.DMA,
                pltpu.SemaphoreType.DMA((2 * SLOTS,)),
                pltpu.SemaphoreType.DMA((4,)),
            ],
        ),
        out_shape=[
            jax.ShapeDtypeStruct((tok, width), bf16),
            jax.ShapeDtypeStruct((tok, width), bf16),
            jax.ShapeDtypeStruct((tok, width), f32),
            jax.ShapeDtypeStruct(vec_rows.shape, f32),
            jax.ShapeDtypeStruct((width, EARLY * width), bf16),
            jax.ShapeDtypeStruct((chips, part, late), bf16),
        ]
        + [jax.ShapeDtypeStruct((4, part, late), bf16)] * 4,
        compiler_params=pltpu.CompilerParams(vmem_limit_bytes=60 * MIB),
        cost_estimate=cost(104),
        name="middle",
    )(where, mixed, tokens, cotangent, vec_rows, packed)


def attend_backward_kernel(
    where_ref, x_ref, q_ref, k_ref, v_ref, mixed_ref, gmixed_ref, probs_ref, share_ref,
    gqkv_ref, gbias_ref, mine_ref, theirs_ref,
    acc, accb, grads_scr, gscr, stage, out_sem,
):
    row = pl.program_id(0)
    length, width = q_ref.shape
    pairs = width // PAIR
    low = lax.broadcasted_iota(jnp.int32, (length, PAIR), 1) < HD
    step = 128
    reach = 256

    @pl.when(row == 0)
    def _():
        acc[...] = jnp.zeros_like(acc)
        accb[...] = jnp.zeros_like(accb)
        grads_scr[...] = jnp.zeros_like(grads_scr)

    heads = -(-width // HD // 8) * 8
    head_of = lax.broadcasted_iota(jnp.int32, (heads, width), 1) // HD
    pick_head = (head_of == lax.broadcasted_iota(jnp.int32, (heads, width), 0)).astype(bf16)
    share = jnp.concatenate([share_ref[0, p] for p in range(pairs)], axis=0)
    if heads > 2 * pairs:
        share = jnp.concatenate([share, jnp.zeros((heads - 2 * pairs, length), f32)], axis=0)
    upper = share.astype(bf16)
    lower = (share - upper.astype(f32)).astype(bf16)
    spread = dot(upper, pick_head, TN) + dot(lower, pick_head, TN)
    scaled = (gmixed_ref[...].astype(f32) * spread).astype(bf16)
    gscr[...] = scaled
    product = scaled.astype(f32) * mixed_ref[...].astype(f32)
    upper = product.astype(bf16)
    lower = (product - upper.astype(f32)).astype(bf16)
    means = dot(pick_head, upper, NT) + dot(pick_head, lower, NT)
    none = jnp.zeros((length, PAIR), bf16)

    for pair in range(pairs):
        at = slice(pair * PAIR, (pair + 1) * PAIR)
        qp, kp, vp, gp = q_ref[:, at], k_ref[:, at], v_ref[:, at], gscr[:, at]
        kt = kp.T
        for side in range(2):
            pick = low if side == 0 else jnp.logical_not(low)
            va = jnp.where(pick, vp, none)
            for b in range(length // step):
                first, last = key_span(b, step, reach, length)
                block = slice(b * step, (b + 1) * step)
                cols = slice(side * length + b * step, side * length + (b + 1) * step)
                gprobs = dot(va[first:last], gp[block], NT)
                head = 2 * pair + side
                grads = probs_ref[0, pair, first:last, cols].astype(f32) * (gprobs - means[head : head + 1, block])
                grads_scr[first:last, cols] = grads.astype(bf16)
        gq_t = jnp.concatenate(
            [dot(kt[:HD], grads_scr[:, :length]), dot(kt[HD:], grads_scr[:, length:])], axis=0
        )
        gq = (gq_t * HD**-0.5).astype(bf16).T
        both_q = jnp.concatenate([jnp.where(low, qp, none), jnp.where(low, none, qp)], axis=0)
        both_g = jnp.concatenate([jnp.where(low, gp, none), jnp.where(low, none, gp)], axis=0)
        gk = dot(grads_scr[...], both_q).astype(bf16)
        gv = dot(probs_ref[0, pair], both_g).astype(bf16)
        for s, part in enumerate((gq, gk, gv)):
            spot = slice(s * width + pair * PAIR, s * width + (pair + 1) * PAIR)
            gqkv_ref[:, spot] = part
            if s != 1:
                accb[:, spot] += fold(part.astype(f32))
    acc[...] += dot(x_ref[...], gqkv_ref[...], TN)

    @pl.when(row == pl.num_programs(0) - 1)
    def _():
        gbias_ref[...] = jnp.broadcast_to(jnp.sum(accb[...], axis=0, keepdims=True), gbias_ref.shape)
        part = stage.shape[1]
        amount = mine_ref.shape[0]

        def send(n, side, dst):
            core = where_ref[1] if side == 0 else 1 - where_ref[1]
            rows = pl.ds(pl.multiple_of((where_ref[2 + n] * 2 + core) * part, 8), part)
            slot = side * amount + n
            stage[slot] = acc[rows, :].astype(bf16)
            pltpu.make_async_copy(stage.at[slot], dst.at[n], out_sem).start()

        def body(n, _):
            send(n, 1, theirs_ref)
            send(n, 0, mine_ref)
            return 0

        lax.fori_loop(0, amount, body, 0)
        pltpu.make_async_copy(stage.at[pl.ds(0, amount)], mine_ref, out_sem).wait()
        pltpu.make_async_copy(stage.at[pl.ds(amount, amount)], theirs_ref, out_sem).wait()


def attend_backward(where, tokens, qkv, mixed, gmixed, probs, share, group, groups):
    rows = probs.shape[0]
    tok, model = tokens.shape
    length = tok // rows
    width = model // groups
    pairs = width // PAIR
    chips = CHIPS
    part = model // (2 * chips)
    any_spec = pl.BlockSpec(memory_space=pl.ANY)
    own = lambda s: pl.BlockSpec((length, width), lambda r, *_: (r, s * groups + group))
    return pl.pallas_call(
        attend_backward_kernel,
        grid_spec=pltpu.PrefetchScalarGridSpec(
            num_scalar_prefetch=1,
            grid=(rows,),
            in_specs=[
                pl.BlockSpec((length, model), lambda r, *_: (r, 0)),
                own(0), own(1), own(2), own(0), own(0),
                pl.BlockSpec((1, pairs, length, 2 * length), lambda r, *_: (r, group, 0, 0)),
                pl.BlockSpec((1, pairs, 2, length), lambda r, *_: (r, group, 0, 0)),
            ],
            out_specs=[
                pl.BlockSpec((length, 3 * width), lambda r, *_: (r, 0)),
                pl.BlockSpec((8, 3 * width), lambda r, *_: (0, 0)),
                any_spec,
                any_spec,
            ],
            scratch_shapes=[
                pltpu.VMEM((model, 3 * width), f32),
                pltpu.VMEM((8, 3 * width), f32),
                pltpu.VMEM((length, 2 * length), bf16),
                pltpu.VMEM((length, width), bf16),
                pltpu.VMEM((2 * chips, part, 3 * width), bf16),
                pltpu.SemaphoreType.DMA,
            ],
        ),
        out_shape=[
            jax.ShapeDtypeStruct((tok, 3 * width), bf16),
            jax.ShapeDtypeStruct((8, 3 * width), f32),
            jax.ShapeDtypeStruct((chips, part, 3 * width), bf16),
            jax.ShapeDtypeStruct((chips, part, 3 * width), bf16),
        ],
        compiler_params=pltpu.CompilerParams(vmem_limit_bytes=56 * MIB),
        cost_estimate=cost(57 // groups),
        name="attend_backward",
    )(where, tokens, qkv, qkv, qkv, mixed, gmixed, probs, share)


def input_grad_kernel(gres_ref, w_ref, *rest):
    parts, out_ref = rest[:-1], rest[-1]
    total = gres_ref[...]
    width = parts[0].shape[1] // 3
    for g, part in enumerate(parts):
        for s in range(3):
            total += dot(part[:, s * width : (s + 1) * width], w_ref[s, :, g * width : (g + 1) * width], NT)
    out_ref[...] = total.astype(bf16)


def input_grad(gres, weights, parts, block=512):
    tok, model = gres.shape
    return pl.pallas_call(
        input_grad_kernel,
        grid=(tok // block,),
        in_specs=[
            pl.BlockSpec((block, model), lambda r: (r, 0)),
            pl.BlockSpec(weights.shape, lambda r: (0, 0, 0)),
        ]
        + [pl.BlockSpec((block, p.shape[1]), lambda r: (r, 0)) for p in parts],
        out_specs=pl.BlockSpec((block, model), lambda r: (r, 0)),
        out_shape=jax.ShapeDtypeStruct((tok, model), bf16),
        compiler_params=pltpu.CompilerParams(vmem_limit_bytes=56 * MIB),
        cost_estimate=cost(0.1),
        name="input_grad",
    )(gres, weights, *parts)


beta_one = 0.5
beta_two = 0.5
adam_eps = 1e-06
decay_rate = 0.01
learn_rate = 0.3
ema_rate = 0.5
ratio_eps = 1e-06
STEP = 7


def whole_sum(v):
    return jnp.sum(jnp.sum(v, axis=0, keepdims=True), axis=1, keepdims=True)


def pack_kernel(up_ref, down_ref, out_w_ref, packed_ref):
    part, width = out_w_ref.shape
    chunks = up_ref.shape[1] // width
    span = 128 * chunks
    place = lax.broadcasted_iota(jnp.int32, (span, span), 0)
    to = lax.broadcasted_iota(jnp.int32, (span, span), 1)
    pick = jnp.where((place % chunks) * 128 + place // chunks == to, 1.0, 0.0).astype(bf16)
    for c in range(width // 128):
        moved = dot(up_ref[:, c * span : (c + 1) * span].astype(bf16), pick).astype(bf16)
        for j in range(chunks):
            packed_ref[:, j * width + c * 128 : j * width + (c + 1) * 128] = moved[:, j * 128 : (j + 1) * 128]
    down = down_ref[...].astype(bf16)
    row = lax.broadcasted_iota(jnp.int32, (part, chunks * part), 0)
    source = lax.broadcasted_iota(jnp.int32, (part, chunks * part), 1)
    for j in range(chunks):
        at = (chunks + j) * width
        pick = jnp.where(source == chunks * row + j, 1.0, 0.0).astype(bf16)
        packed_ref[:, at : at + width] = dot(pick, down).astype(bf16)
    packed_ref[:, 2 * chunks * width :] = out_w_ref[...].astype(bf16)


def pack(w_out, w_up, w_down):
    part, width = w_out.shape
    return pl.pallas_call(
        pack_kernel,
        out_shape=jax.ShapeDtypeStruct((part, 2 * w_up.shape[1] + width), bf16),
        compiler_params=pltpu.CompilerParams(vmem_limit_bytes=56 * MIB),
        cost_estimate=cost(2),
        name="pack",
    )(w_up, w_down, w_out)


def spread_vec(vec, part):
    return jnp.concatenate([vec[:, c * 128 : (c + 1) * 128] for c in range(vec.shape[1] // 128)], axis=0)


def joined_vec(rows):
    return jnp.concatenate([rows[16 * c : 16 * c + 16] for c in range(rows.shape[0] // 16)], axis=1)


def near_kernel(mine_ref, came_ref, vec_ref, vec_came_ref, *sent_refs):
    part, width = mine_ref.shape[1:]
    vec = spread_vec(vec_ref[...] + vec_came_ref[...], part)
    for xy in range(3):
        for z in range(4):
            at = 4 * xy + 4 + z
            sent_refs[xy][z, :, :width] = (mine_ref[at].astype(f32) + came_ref[at].astype(f32)).astype(bf16)
            sent_refs[xy][z, :, width:] = vec[z * part : (z + 1) * part].astype(bf16)


def near(mine, came, vec, vec_came):
    chips, part, width = mine.shape
    return pl.pallas_call(
        near_kernel,
        out_shape=[jax.ShapeDtypeStruct((4, part, width + 128), bf16)] * 3,
        compiler_params=pltpu.CompilerParams(vmem_limit_bytes=56 * MIB),
        cost_estimate=cost(0.1),
        name="near",
    )(mine, came, vec, vec_came)


def line_kernel(with_vec, *refs):
    mine_ref, came_ref = refs[:2]
    parts = refs[2:5]
    refs = refs[5:]
    if with_vec:
        vec_ref, vec_came_ref = refs[:2]
        refs = refs[2:]
    part, width = mine_ref.shape[1:]
    if with_vec:
        vec = spread_vec(vec_ref[...] + vec_came_ref[...], part)
        blocks = []
        for z in range(4):
            block = vec[z * part : (z + 1) * part]
            for p in parts:
                block = block + p[z, :, width:].astype(f32)
            blocks.append(block)
        low = jnp.concatenate(blocks, axis=1).astype(bf16)
        refs[4][...] = joined_vec(jnp.concatenate(blocks, axis=0))
    for z in range(4):
        rows = mine_ref[z].astype(f32) + came_ref[z].astype(f32)
        for p in parts:
            rows = rows + p[z, :, :width].astype(f32)
        if z == 0:
            refs[0][...] = rows
        else:
            refs[z][:, :width] = rows.astype(bf16)
            if with_vec:
                refs[z][:, width:] = low


def line(mine, came, parts, vecs=()):
    chips, part, width = mine.shape
    wide = width + (512 if vecs else 0)
    full = lambda a: pl.BlockSpec(a.shape, lambda i: (0,) * a.ndim)
    first = pl.BlockSpec((4, part, width), lambda i: (0, 0, 0))
    shapes = [jax.ShapeDtypeStruct((part, width), f32)] + [jax.ShapeDtypeStruct((part, wide), bf16)] * 3
    if vecs:
        shapes.append(jax.ShapeDtypeStruct(vecs[0].shape, f32))
    return pl.pallas_call(
        functools.partial(line_kernel, bool(vecs)),
        grid=(1,),
        in_specs=[first, first] + [full(p) for p in parts] + [full(v) for v in vecs],
        out_specs=[full(o) for o in shapes],
        out_shape=shapes,
        compiler_params=pltpu.CompilerParams(vmem_limit_bytes=56 * MIB),
        cost_estimate=cost(0.1),
        name="line",
    )(mine, came, *parts, *vecs)


def own_grads_kernel(amount, where_ref, rows_ref, vec_ref, *refs):
    parts = refs[:amount]
    gq_ref, gv_ref, gb_ref = refs[amount:]
    part, width = rows_ref.shape
    model = width // 3
    rows = rows_ref[...]
    for p in parts:
        rows = rows + p[:, :width].astype(f32)
    for s in range(3):
        gq_ref[s] = rows[:, s * model : (s + 1) * model]
    vec = vec_ref[...]
    if amount:
        blocks = []
        for z in range(4):
            block = jnp.zeros((part, 128), f32)
            for p in parts:
                block = block + p[:, width + z * 128 : width + (z + 1) * 128].astype(f32)
            blocks.append(block)
        vec = vec + joined_vec(jnp.concatenate(blocks, axis=0))
    first = where_ref[0] * part
    chunks = gb_ref.shape[1] // part

    def picked(values, count, repeat):
        place = lax.broadcasted_iota(jnp.int32, (model, count), 0)
        wanted = first + lax.broadcasted_iota(jnp.int32, (model, count), 1) // repeat
        pick = jnp.where(place == wanted, 1.0, 0.0)
        return lax.dot_general(values, pick, NN, precision=lax.Precision.HIGHEST, preferred_element_type=f32)

    gv_ref[...] = picked(vec[0:8], part, 1)
    spread = picked(vec[8:16], chunks * part, chunks)
    row = lax.broadcasted_iota(jnp.int32, spread.shape, 0)
    lane = lax.broadcasted_iota(jnp.int32, spread.shape, 1)
    gb_ref[...] = jnp.sum(jnp.where(lane % chunks == row, spread, 0.0), axis=0, keepdims=True)


def own_grads(index, rows, vec, parts, chunks):
    part, width = rows.shape
    model = width // 3
    spec = pl.BlockSpec(memory_space=pltpu.VMEM)
    return pl.pallas_call(
        functools.partial(own_grads_kernel, len(parts)),
        in_specs=[pl.BlockSpec(memory_space=pltpu.SMEM)] + [spec] * (2 + len(parts)),
        out_specs=[spec] * 3,
        out_shape=[
            jax.ShapeDtypeStruct((3, part, model), f32),
            jax.ShapeDtypeStruct((8, part), f32),
            jax.ShapeDtypeStruct((1, chunks * part), f32),
        ],
        compiler_params=pltpu.CompilerParams(vmem_limit_bytes=56 * MIB),
        cost_estimate=cost(0.1),
        name="own_grads",
    )(index, rows, vec, *parts)


def moments_kernel(kinds, *refs):
    n = len(kinds)
    grads, masters, firsts, seconds = (refs[i * n : (i + 1) * n] for i in range(4))
    new_firsts, new_seconds, updates = (refs[(4 + i) * n : (5 + i) * n] for i in range(3))
    squares_ref = refs[7 * n]
    lane = lax.broadcasted_iota(jnp.int32, squares_ref.shape, 1)
    row = lax.broadcasted_iota(jnp.int32, squares_ref.shape, 0)
    squares = jnp.zeros(squares_ref.shape, f32)
    corr_one = 1.0 - beta_one**STEP
    corr_two = 1.0 - beta_two**STEP
    for i, (spot, amount) in enumerate(kinds):
        grad = grads[i][...]
        master = masters[i][...]
        first = beta_one * firsts[i][...] + (1.0 - beta_one) * grad
        second = beta_two * seconds[i][...] + (1.0 - beta_two) * grad * grad
        update = first / corr_one / (jnp.sqrt(second / corr_two) + adam_eps) + decay_rate * master
        new_firsts[i][...] = first
        new_seconds[i][...] = second
        updates[i][...] = update
        for k in range(amount):
            if amount == 1:
                pair = (master, update)
            elif len(master.shape) == 3:
                pair = (master[k], update[k])
            else:
                pair = (master[k : k + 1], update[k : k + 1])
            for r, v in enumerate(pair):
                squares = jnp.where((lane == spot + k) & (row == r), whole_sum(v * v), squares)
    squares_ref[...] = squares


def moments(kinds, grads, masters, firsts, seconds):
    shapes = [jax.ShapeDtypeStruct(m.shape, f32) for m in masters]
    n = len(kinds)
    out = pl.pallas_call(
        functools.partial(moments_kernel, kinds),
        out_shape=shapes * 3 + [jax.ShapeDtypeStruct((8, 128), f32)],
        compiler_params=pltpu.CompilerParams(vmem_limit_bytes=56 * MIB),
        cost_estimate=cost(0.1),
        name="moments",
    )(*grads, *masters, *firsts, *seconds)
    return out[:n], out[n : 2 * n], out[2 * n : 3 * n], out[3 * n]


def renew_kernel(kinds, came_ref, *refs):
    n = len(kinds)
    masters, updates, averages = (refs[i * n : (i + 1) * n] for i in range(3))
    news, emas, copies = (refs[(3 + i) * n : (4 + i) * n] for i in range(3))
    norm_ref, ratio_ref = refs[6 * n :]
    total = jnp.sum(came_ref[...], axis=0)
    norms = jnp.sqrt(total)
    ratios = norms[0:1] / jnp.sqrt(total[1:2] + ratio_eps)
    norm_ref[...] = norms[0:2, : norm_ref.shape[1]]
    ratio_ref[...] = ratios[:, : ratio_ref.shape[1]]
    lane = lax.broadcasted_iota(jnp.int32, ratios.shape, 1)
    for i, (spot, amount) in enumerate(kinds):
        for k in range(amount):
            at = ... if amount == 1 else (k if len(masters[i].shape) == 3 else slice(k, k + 1))
            ratio = jnp.sum(jnp.where(lane == spot + k, ratios, 0.0), axis=1, keepdims=True)
            new = masters[i][at] - learn_rate * ratio * updates[i][at]
            news[i][at] = new
            emas[i][at] = ema_rate * averages[i][at] + (1.0 - ema_rate) * new
            copies[i][at] = new.astype(bf16)


def renew(kinds, came, masters, updates, averages):
    shapes = [jax.ShapeDtypeStruct(m.shape, f32) for m in masters]
    halves = [jax.ShapeDtypeStruct(m.shape, bf16) for m in masters]
    n = len(kinds)
    out = pl.pallas_call(
        functools.partial(renew_kernel, kinds),
        out_shape=shapes * 2 + halves + [jax.ShapeDtypeStruct((2, 15), f32), jax.ShapeDtypeStruct((1, 15), f32)],
        compiler_params=pltpu.CompilerParams(vmem_limit_bytes=56 * MIB),
        cost_estimate=cost(0.1),
        name="renew",
    )(came, *masters, *updates, *averages)
    return out[:n], out[n : 2 * n], out[2 * n : 3 * n], out[3 * n], out[3 * n + 1].reshape(15)


class Ring:
    def __init__(self, sizes):
        self.sizes = sizes
        self.amount = sizes["gx"] * sizes["gy"]
        self.near = sizes == {"gx": 8, "gy": 4}

    def index(self):
        return lax.axis_index("gx") * self.sizes["gy"] + lax.axis_index("gy")

    def swap(self, value, bits):
        return lax.ppermute(value, ALL, [(i, i ^ bits) for i in range(self.amount)])

    def core(self, value):
        return self.swap(value, 1)

    def plane(self, value, k):
        return self.swap(value, k << 1)

    def line(self, value, k):
        return self.swap(value, k << 3)


def where_am_i(ring):
    if not ring.near:
        return jnp.asarray([0, 0] + list(range(CHIPS)), jnp.int32)
    me = ring.index()
    chip = me // 2
    order = [chip ^ ((z << 2) | xy) for xy in range(4) for z in range(4)]
    return jnp.stack([chip, me % 2] + order).astype(jnp.int32)


def gather_first(ring, w_qkv, vec_part):
    low = w_qkv.astype(bf16)
    part, width = low.shape[1], low.shape[2]
    half = width // 2
    vec_rows = vec_part.shape[0]
    vec_part = vec_part.astype(bf16)
    if not ring.near:
        full = lax.all_gather(low, ALL, axis=1, tiled=True)
        blocks = full.reshape(3, CHIPS, width // CHIPS, 2, half).transpose(3, 1, 0, 2, 4)
        blocks = blocks.reshape(8, 4 * 3 * width // CHIPS, half)
        vecs = lax.all_gather(vec_part, ALL, axis=1, tiled=True)
        return [blocks[i] for i in range(8)], vecs.astype(f32)
    me = ring.index()
    core = me % 2
    spread = jnp.zeros((16, width), bf16)
    spread = lax.dynamic_update_slice(spread, vec_part, (0, me * part))
    spread = spread.reshape(32, half)
    left, right = low[:, :, :half], low[:, :, half:]
    keep = jnp.where(core == 0, left, right)
    give = jnp.where(core == 0, right, left)
    got = ring.core(jnp.concatenate([give.reshape(3 * part, half), spread], axis=0))
    came = got[: 3 * part].reshape(3, part, half)
    block = jnp.where(
        core == 0, jnp.concatenate([keep, came], axis=1), jnp.concatenate([came, keep], axis=1)
    ).reshape(6 * part, half)
    payload = jnp.concatenate([block, spread + got[3 * part :]], axis=0)
    cut = 6 * part
    lines = [payload] + [ring.line(payload, k) for k in (1, 2, 3)]
    total = lines[0][cut:] + lines[1][cut:] + lines[2][cut:] + lines[3][cut:]
    payload = jnp.concatenate([v[:cut] for v in lines] + [total], axis=0)
    mine = [payload] + [ring.plane(payload, k) for k in (1, 2, 3)]
    theirs = [ring.core(v) for v in mine]
    cut = 4 * cut
    total = mine[0][cut:] + mine[1][cut:] + mine[2][cut:] + mine[3][cut:]
    return mine + theirs, total.reshape(16, width)[:vec_rows].astype(f32)


def gather_rest(w_out, w_up, w_down):
    packed = pack(w_out, w_up, w_down)
    return lax.all_gather(packed, ALL, axis=0, tiled=True)


def after(value, *others):
    return lax.optimization_barrier((value,) + others)[0]


def scatter_far(mine, theirs):
    chips, part, width = mine.shape
    full = jnp.stack([mine, theirs], axis=1).reshape(2 * chips * part, width)
    return lax.psum_scatter(full, ALL, scatter_dimension=0, tiled=True).astype(f32)


def share(ring, squares):
    if not ring.near:
        return lax.psum(squares, ALL)[None]
    return lax.all_to_all(jnp.broadcast_to(squares[None], (ring.amount,) + squares.shape), ALL, 0, 0)


def on_device(
    ring,
    tokens,
    seg_lengths,
    cotangent,
    *params,
):
    masters = params[0:6]
    averages = params[18:24]
    w_qkv, w_out, w_up, w_down, vecs, b_up = masters
    part, width = w_out.shape
    chunks = w_up.shape[1] // width
    bounds = jnp.stack(
        [jnp.sum(seg_lengths[:, : k + 1], axis=1) for k in range(seg_lengths.shape[1])], axis=1
    ).astype(jnp.int32)
    where = where_am_i(ring)
    packed = gather_rest(w_out, w_up, w_down)
    vec_part = jnp.concatenate([vecs, b_up.reshape(part, chunks).T], axis=0)
    raws, vec_rows = gather_first(ring, w_qkv, vec_part)
    vec_rows = jnp.concatenate([vec_rows, jnp.zeros((4, width), f32)], axis=0)
    qkv, mixed, probs, share_rows, full_qkv = attend_forward(where, bounds, tokens, vec_rows, raws)
    layer_out, gmixed, gres, gvec, down, mine, *theirs = middle(
        where, mixed, tokens, cotangent, vec_rows, packed
    )
    down = lax.psum_scatter(down, ALL, scatter_dimension=0, tiled=True)
    firsts_in = list(params[6:12])
    seconds_in = list(params[12:18])

    def join_vec(gvec, gbias):
        gbias = gbias[0].reshape(3, width)
        return jnp.concatenate([gbias[0:1], gbias[2:3], gvec[2:]], axis=0)

    if ring.near:
        came = [None] * 4
        for k in (1, 2, 3, 0):
            came[k] = ring.core(theirs[k])
        sent = []
        for k in (1, 2, 3):
            other = after(came[k], *sent)
            sent.append((mine[4 * k : 4 * k + 4].astype(f32) + other.astype(f32)).astype(bf16))
        parts = [ring.plane(v, k + 1) for k, v in enumerate(sent)]
        gate = after(gmixed, came[0], *sent)
        gqkv, gbias, mine_q, theirs_q = attend_backward(where, tokens, qkv, mixed, gate, probs, share_rows, 0, 1)
        gvec = join_vec(gvec, after(gbias, *parts))
        came_q = ring.core(after(theirs_q, *parts))
        vec_came = ring.core(gvec)
        sent_q = near(mine_q, came_q, gvec, vec_came)
        parts_q = [ring.plane(v, k + 1) for k, v in enumerate(sent_q)]
        parts[0] = after(parts[0], *sent_q)
        rows, *sent = line(mine, came[0], parts)
        grad_input = input_grad(after(gres, *sent, *sent_q), full_qkv, [gqkv])
        sent[2] = after(sent[2], grad_input)
        parts = [ring.line(v, k + 1) for k, v in enumerate(sent)]
        parts_q[0] = after(parts_q[0], grad_input, parts[0], parts[1])
        rows_q, *sent_q, vec_q = line(mine_q, came_q, parts_q, (gvec, vec_came))
        parts_q = [ring.line(v, k + 1) for k, v in enumerate(sent_q)]
        rows = after(rows, *sent_q)
        down = after(down, *sent_q)
        grad_rest = rows + parts[0].astype(f32) + parts[1].astype(f32) + parts[2].astype(f32)
    else:
        gqkv, gbias, mine_q, theirs_q = attend_backward(where, tokens, qkv, mixed, gmixed, probs, share_rows, 0, 1)
        grad_input = input_grad(gres, full_qkv, [gqkv])
        grad_rest = scatter_far(mine, jnp.concatenate(theirs, axis=0))
        rows_q, vec_q, parts_q = scatter_far(mine_q, theirs_q), lax.psum(join_vec(gvec, gbias), ALL), []
    ff = chunks * width
    kinds = ((3, 1), (4, 1), (5, 1))
    grad_down = jnp.concatenate([down.astype(f32), grad_rest[:, ff + width :]], axis=1)
    grads = (
        grad_rest[:, ff : ff + width],
        grad_rest[:, :ff].reshape(part, chunks, width).transpose(0, 2, 1).reshape(part, ff),
        grad_down.reshape(part * chunks, width),
    )
    firsts_r, seconds_r, updates_r, squares_r = moments(
        kinds, grads, masters[1:4], firsts_in[1:4], seconds_in[1:4]
    )
    if parts_q:
        parts_q[0] = after(parts_q[0], squares_r)
    index = ring.index().reshape(1).astype(jnp.int32)
    grads = own_grads(index, rows_q, vec_q, parts_q, chunks)
    flat = lambda v: v.reshape(1, -1)
    pick = lambda v: (v[0], v[4], flat(v[5]))
    others = ((0, 3), (6, 8), (14, 1))
    firsts_q, seconds_q, updates_q, squares_q = moments(
        others, grads, pick(masters), pick(firsts_in), pick(seconds_in)
    )
    came = share(ring, squares_r + squares_q)
    news, emas, copies, norms, ratios = renew(
        kinds + others,
        came,
        tuple(masters[1:4]) + pick(masters),
        tuple(updates_r) + tuple(updates_q),
        tuple(averages[1:4]) + pick(averages),
    )
    order = lambda v: (v[3], v[0], v[1], v[2], v[4], v[5].reshape(-1))
    out = [layer_out, grad_input]
    for found in (news, list(firsts_r) + list(firsts_q), list(seconds_r) + list(seconds_q), emas, copies):
        out.extend(order(found))
    return (*out, ratios, norms)


def solution(mesh):
    ring = Ring(dict(mesh.shape))
    rows = P(ALL, None)
    kinds = (P(None, ALL, None), rows, rows, rows, P(None, ALL), P(ALL))
    return jax.shard_map(
        functools.partial(on_device, ring),
        mesh=mesh,
        in_specs=(rows, rows, rows) + kinds * 4,
        out_specs=(rows, rows) + kinds * 5 + (P(), P()),
        check_vma=False,
    )
```
